256 devices in a mesh: sector: 8 (over z), rows: 32 (over x, y, core).
Axes of the slice: x: 4, y: 4, z: 8, core: 2. Of those that a mesh axis runs over, the one named last changes fastest.
Arguments:
- x_block: bfloat16 [8, 40960, 300], P('sector', 'rows')
- h_diag: bfloat16 [8, 40960, 1280], P('sector', 'rows')
- h_right: bfloat16 [8, 40960, 1280], P('sector', 'rows')
- pattern: int32 [8, 2, 320, 10], P('sector', None, 'rows'), may hold values from 0 to 1, as said below
Outputs:
- q_block: bfloat16 [8, 40960, 300], P('sector', 'rows')
- hproj: float32 [8, 300, 300], P('sector')
- correlation: float32 [8, 300, 300], P('sector')
The draws below stay inside these ranges and needn't reach their ends.
Inputs may be any that keep to these rules, and one draw needn't show every extreme that they name: Within each 1280 x 1280 tile, pattern[s, 0] is symmetric with ones on its diagonal; h_diag's tiles are symmetric.
All inputs are finite; a program needn't handle non-finite values.
Results may differ from the reference program's by a relative error of at most 0.011.
Values may be sent and summed in bfloat16 or wider, within the bound.
A program may use at most 64 MiB of HBM per device.

```python
import math
import jax
import jax.numpy as jnp
from jax import lax

CHANNELS = 300
SUBBLOCK = 128
BLOCK_ROWS = 1280
NROWS = 40960
SECTORS = 8


def noise_field(key, shape):
    return jax.random.normal(key, shape, jnp.float32)


def draw_x_block(key, part):
    common = noise_field(jax.random.fold_in(key, 11), (1, NROWS, CHANNELS))
    own = noise_field(jax.random.fold_in(key, 12), (SECTORS, NROWS, CHANNELS))
    shared = noise_field(jax.random.fold_in(key, 14), (SECTORS, NROWS, 1))
    values = common + 0.6 * own + 0.5 * shared
    return jnp.clip(values, -6.0, 6.0).astype(jnp.bfloat16)


def coupling_field(key):
    common = noise_field(jax.random.fold_in(key, 21), (1, NROWS, BLOCK_ROWS))
    own = noise_field(jax.random.fold_in(key, 22), (SECTORS, NROWS, BLOCK_ROWS))
    return (common + 0.6 * own) * (0.8 / math.sqrt(BLOCK_ROWS))


def draw_h_diag(key, part):
    count = NROWS // BLOCK_ROWS
    raw = coupling_field(jax.random.fold_in(key, 31)).reshape(SECTORS, count, BLOCK_ROWS, BLOCK_ROWS)
    sym = (raw + jnp.swapaxes(raw, 2, 3)) * (1.0 / math.sqrt(2.0))
    lower, upper = (5.0, 10.0)
    base = jnp.exp(jax.random.uniform(jax.random.fold_in(key, 32), (1, count, BLOCK_ROWS, 1), jnp.float32, math.log(lower), math.log(upper)))
    shift = jax.random.uniform(jax.random.fold_in(key, 33), (SECTORS, count, BLOCK_ROWS, 1), jnp.float32, 0.9, 1.1)
    eye = jnp.eye(BLOCK_ROWS, dtype=jnp.float32)
    tiles = sym + base * shift * eye
    return tiles.reshape(SECTORS, NROWS, BLOCK_ROWS).astype(jnp.bfloat16)


def draw_h_right(key, part):
    return coupling_field(jax.random.fold_in(key, 41)).astype(jnp.bfloat16)


def draw_pattern(key, part):
    count = NROWS // BLOCK_ROWS
    width = BLOCK_ROWS // SUBBLOCK
    bits = jax.random.randint(jax.random.fold_in(key, 51), (SECTORS, 2, count, width, width), 0, 2)
    first = bits[:, 0]
    first = jnp.maximum(first, jnp.swapaxes(first, 2, 3))
    first = jnp.maximum(first, jnp.eye(width, dtype=jnp.int32))
    both = jnp.stack([first, bits[:, 1]], axis=1)
    return both.reshape(SECTORS, 2, count * width, width).astype(jnp.int32)


def setup_inputs(seed: int = 0) -> dict:
    keys = jax.random.split(jax.random.key(seed), 5)
    x_block = draw_x_block(jax.random.fold_in(keys[4], 71), 0)
    h_diag = draw_h_diag(jax.random.fold_in(keys[4], 71), 0)
    h_right = draw_h_right(jax.random.fold_in(keys[4], 71), 0)
    pattern = draw_pattern(jax.random.fold_in(keys[4], 71), 0)
    return dict(x_block=x_block, h_diag=h_diag, h_right=h_right, pattern=pattern)


def expand(blocks):
    return jnp.repeat(jnp.repeat(blocks, SUBBLOCK, axis=-2), SUBBLOCK, axis=-1)

def sector_image(inputs, diag_rows, right_rows, masks):
    count = NROWS // BLOCK_ROWS
    width = BLOCK_ROWS // SUBBLOCK
    starts = inputs.reshape(count, BLOCK_ROWS, CHANNELS).astype(jnp.float32)
    mask_diag = expand(masks[0].reshape(count, width, width)).astype(jnp.bfloat16)
    mask_right = expand(masks[1].reshape(count, width, width)).astype(jnp.bfloat16)
    diag_tile = (diag_rows.reshape(count, BLOCK_ROWS, BLOCK_ROWS) * mask_diag).astype(jnp.float32)
    right_tile = (right_rows.reshape(count, BLOCK_ROWS, BLOCK_ROWS) * mask_right).astype(jnp.float32)
    empty = jnp.zeros((1, BLOCK_ROWS, CHANNELS), jnp.float32)
    later = jnp.concatenate([starts[1:], empty], axis=0)
    first = jnp.einsum('bij,bjk->bik', diag_tile, starts)
    second = jnp.einsum('bij,bjk->bik', right_tile, later)
    carried = jnp.einsum('bji,bjk->bik', right_tile, starts)
    third = jnp.concatenate([empty, carried[:-1]], axis=0)
    image = first + second + third
    return image.reshape(NROWS, CHANNELS).astype(jnp.bfloat16)

def reference(x_block, h_diag, h_right, pattern):
    bases = []
    projected = []
    correlations = []
    eye = jnp.eye(CHANNELS, dtype=jnp.float32)
    for sector_num in range(SECTORS):
        inputs = x_block[sector_num]
        image = sector_image(inputs, h_diag[sector_num], h_right[sector_num], pattern[sector_num])
        gram = jnp.dot(image.T.astype(jnp.float32), image.astype(jnp.float32), preferred_element_type=jnp.float32) / NROWS
        rayleigh = jnp.dot(inputs.T.astype(jnp.float32), image.astype(jnp.float32), preferred_element_type=jnp.float32) / NROWS
        factor = jnp.linalg.cholesky(gram)
        inverse = jax.scipy.linalg.solve_triangular(factor, eye, lower=True)
        basis = jnp.dot(image.astype(jnp.float32), inverse.T, precision=lax.Precision.HIGH).astype(jnp.bfloat16)
        if sector_num == 0:
            correlations.append(jnp.zeros((CHANNELS, CHANNELS), jnp.float32))
        else:
            correlations.append(jnp.dot(bases[-1].T.astype(jnp.float32), basis.astype(jnp.float32), preferred_element_type=jnp.float32) / NROWS)
        bases.append(basis)
        projected.append(rayleigh)
    return (jnp.stack(bases), jnp.stack(projected), jnp.stack(correlations))
```

```python
import jax
import jax.numpy as jnp
from jax import lax
from jax.experimental import pallas as pl
from jax.experimental.pallas import tpu as pltpu
from jax.sharding import PartitionSpec as P

HI = lax.Precision.HIGHEST
MESH = pl.DeviceIdType.MESH
F32 = jnp.float32
BF16 = jnp.bfloat16
N = 304
LANES = 384
C = 300
ROWS = 1280
CHUNK = 256
NCH = ROWS // CHUNK
BLOCK = 128


def nt(a, b, precision=None):
    return lax.dot_general(a, b, (((1,), (1,)), ((), ())), precision=precision, preferred_element_type=F32)


def tn(a, b, precision=None):
    return lax.dot_general(a, b, (((0,), (0,)), ((), ())), precision=precision, preferred_element_type=F32)


def nn(a, b, precision=None):
    return lax.dot_general(a, b, (((1,), (0,)), ((), ())), precision=precision, preferred_element_type=F32)


def panel_block(tiles, base_lane, count):
    lane = lax.broadcasted_iota(jnp.int32, (8, 128), 1)
    sub = lax.broadcasted_iota(jnp.int32, (8, 128), 0)
    ntile = len(tiles[0])
    for k in range(count):
        lo = 8 * k
        inside = (lane >= lo) & (lane < lo + 8)
        P = tiles[k]
        rows = [[jnp.broadcast_to(P[t][q:q + 1, :], (8, 128)) for t in range(ntile)] for q in range(8)]
        s = [[jnp.broadcast_to(rows[q][0][:, lo + p:lo + p + 1], (8, 128)) if p >= q else None for p in range(8)] for q in range(8)]
        for q in range(8):
            rows[q][0] = jnp.where(inside, jnp.where(lane == lo + q, 1.0, 0.0), rows[q][0])
        u = [[None] * 8 for _ in range(8)]
        rs = [None] * 8
        for p in range(8):
            rs[p] = lax.rsqrt(s[p][p])
            for r in range(p + 1, 8):
                u[p][r] = s[p][r] * rs[p]
            for q in range(p + 1, 8):
                for r in range(q, 8):
                    s[q][r] = s[q][r] - u[p][q] * u[p][r]
            rows[p] = [x * rs[p] for x in rows[p]]
            for q in range(p + 1, 8):
                rows[q] = [x - u[p][q] * y for x, y in zip(rows[q], rows[p])]
        fin = []
        for t in range(ntile):
            acc = rows[0][t]
            for q in range(1, 8):
                acc = jnp.where(sub == q, rows[q][t], acc)
            fin.append(acc)
        tiles[k] = fin
        for g in range(k + 1, count):
            cols = []
            for p in range(8):
                c = jnp.broadcast_to(tiles[g][0][:, lo + p:lo + p + 1], (8, 128))
                for q in range(p):
                    c = c - cols[q] * u[q][p]
                cols.append(c * rs[p])
            new = list(tiles[g])
            new[0] = jnp.where(inside, 0.0, new[0])
            for t in range(ntile):
                acc = new[t]
                for p in range(8):
                    acc = acc - cols[p] * rows[p][t]
                new[t] = acc
            tiles[g] = new
    return tiles

def chol_body(w):
    lane3 = None
    for b, cnt in ((0, 16), (1, 16), (2, 6)):
        r0 = 128 * b
        order = [b] + [t for t in range(3) if t != b]
        tiles = [[w[t, r0 + 8 * g:r0 + 8 * g + 8, :] for t in order] for g in range(cnt)]
        tiles = panel_block(tiles, r0, cnt)
        for g in range(cnt):
            for i, t in enumerate(order):
                w[t, r0 + 8 * g:r0 + 8 * g + 8, :] = tiles[g][i]
        r1 = r0 + 8 * cnt
        if r1 < N:
            m = N - r1
            left = jnp.concatenate([w[t, r0:r1, :] for t in range(b + 1, 3)], axis=1)[:, :]
            for t in range(3):
                right = w[t, r0:r1, :]
                if t == b:
                    size = r1 - r0
                    right = jnp.where(lax.broadcasted_iota(jnp.int32, (size, 128), 1) <= lax.broadcasted_iota(jnp.int32, (size, 128), 0), right, 0.0)
                upd = lax.dot_general(left, right, (((0,), (0,)), ((), ())), precision=HI, preferred_element_type=jnp.float32)[:m]
                if t == b:
                    w[t, r1:N, :] = -upd
                else:
                    w[t, r1:N, :] = w[t, r1:N, :] - upd


def iota(shape, dim):
    return lax.broadcasted_iota(jnp.int32, shape, dim)


def pack_symmetric(full, out):
    corner = pltpu.roll(full[256:304, 256:384], 0, 1)
    out[0:80, :] = full[0:80, 0:128]
    low = full[80:128, 0:128]
    out[80:128, :] = jnp.where(iota((48, 128), 1) < 48, corner, low)
    out[128:256, :] = full[0:128, 128:256]
    out[256:384, :] = full[128:256, 128:256]
    out[384:512, :] = full[0:128, 256:384] + pltpu.roll(full[128:256, 256:384], 64, 1)


def unpack_upper(packed):
    top = packed[0:128, :]
    upper = iota((128, 128), 1) >= iota((128, 128), 0)
    b00 = jnp.where(upper, top, top.T)
    b22 = jnp.where(iota((48, 128), 1) < 44, top[80:128, :], 0.0)
    both = packed[384:512, :]
    left = iota((128, 128), 1) < 64
    b02 = jnp.where(left, both, 0.0)
    b12 = jnp.where(left, pltpu.roll(both, 64, 1), 0.0)
    return b00, packed[128:256, :], packed[256:384, :], b02, b12, b22


def exchange_sum(me, sector, count, part, recv, total, sems, scale):
    send, arrive, send2, arrive2 = sems
    size = part.shape[0] // count

    def rows_of(index):
        return pl.ds(pl.multiple_of(index * size, 8), size)

    def first(k):
        peer = lax.rem(me + k, count)
        return pltpu.make_async_remote_copy(
            src_ref=part.at[rows_of(peer)], dst_ref=recv.at[k], send_sem=send.at[k], recv_sem=arrive.at[k],
            device_id=(sector, peer), device_id_type=MESH)

    def second(k):
        peer = lax.rem(me + k, count)
        return pltpu.make_async_remote_copy(
            src_ref=total.at[rows_of(me)], dst_ref=total.at[rows_of(me)], send_sem=send2.at[k],
            recv_sem=arrive2.at[k], device_id=(sector, peer), device_id_type=MESH)

    def start1(k, carry):
        first(k).start()
        return carry

    def sum1(k, acc):
        first(k).wait_recv()
        return acc + recv[k]

    def start2(k, carry):
        second(k).start()
        return carry

    def wait2(k, carry):
        second(k).wait_recv()
        return carry

    def drain(k, carry):
        first(k).wait_send()
        second(k).wait_send()
        return carry

    lax.fori_loop(1, count, start1, 0)
    acc = lax.fori_loop(1, count, sum1, part[rows_of(me), :])
    total[rows_of(me), :] = acc * scale
    lax.fori_loop(1, count, start2, 0)
    return lambda: (lax.fori_loop(1, count, wait2, 0), lax.fori_loop(1, count, drain, 0))


def greet(me, sector, count):
    barrier = pltpu.get_barrier_semaphore()

    def signal(k, carry):
        pl.semaphore_signal(barrier, inc=1, device_id=(sector, lax.rem(me + k, count)), device_id_type=MESH)
        return carry

    lax.fori_loop(1, count, signal, 0)
    return barrier


def front_kernel(count, pattern, x_hbm, d_hbm, r_hbm, y_out, s_out,
                 xv, xn, dv, rv, acc, cs, cr, full, part, recv, total,
                 load, xsend, xrecv, csend, crecv, s1, s2, s3, s4):
    me = lax.axis_index("rows")
    sector = lax.axis_index("sector")
    loads = [pltpu.make_async_copy(x_hbm, xv, load.at[0])]
    for c in range(NCH):
        cols = pl.ds(c * CHUNK, CHUNK)
        loads.append(pltpu.make_async_copy(r_hbm.at[:, cols], rv.at[:, cols], load.at[1 + c]))
    for c in range(NCH):
        cols = pl.ds(c * CHUNK, CHUNK)
        loads.append(pltpu.make_async_copy(d_hbm.at[:, cols], dv.at[:, cols], load.at[1 + NCH + c]))
    for l in loads:
        l.start()
    barrier = greet(me, sector, count)
    pl.semaphore_wait(barrier, count - 1)

    def x_copy(c):
        cols = pl.ds(c * CHUNK, CHUNK)
        return pltpu.make_async_remote_copy(
            src_ref=x_hbm.at[:, cols], dst_ref=xn.at[:, cols], send_sem=xsend.at[c], recv_sem=xrecv.at[c],
            device_id=(sector, me - 1), device_id_type=MESH)

    def c_copy(c):
        cols = pl.ds(c * CHUNK, CHUNK)
        return pltpu.make_async_remote_copy(
            src_ref=cs.at[:, cols], dst_ref=cr.at[:, cols], send_sem=csend.at[c], recv_sem=crecv.at[c],
            device_id=(sector, me + 1), device_id_type=MESH)

    @pl.when(me > 0)
    def _():
        for c in range(NCH):
            x_copy(c).start()

    full[...] = jnp.zeros((N, LANES), F32)

    def mask(tile, which, c):
        for i in range(ROWS // BLOCK):
            for j in range(CHUNK // BLOCK):
                row = slice(i * BLOCK, (i + 1) * BLOCK)
                col = slice(c * CHUNK + j * BLOCK, c * CHUNK + (j + 1) * BLOCK)
                keep = pattern[i, which, c * (CHUNK // BLOCK) + j]
                scale = jnp.full((BLOCK, BLOCK), keep.astype(F32)).astype(BF16)
                tile[row, col] = tile[row, col] * scale

    loads[0].wait()
    for c in range(NCH):
        cols = slice(c * CHUNK, (c + 1) * CHUNK)
        loads[1 + c].wait()
        mask(rv, 1, c)
        cs[:, cols] = nn(xv[...], rv[:, cols]).astype(BF16)

        @pl.when(me < count - 1)
        def _():
            c_copy(c).start()

    for c in range(NCH):
        cols = slice(c * CHUNK, (c + 1) * CHUNK)
        loads[1 + NCH + c].wait()
        mask(dv, 0, c)
        acc[:, cols] = nn(xv[...], dv[:, cols])

    for c in range(NCH):
        @pl.when(me < count - 1)
        def _():
            cols = slice(c * CHUNK, (c + 1) * CHUNK)
            x_copy(c).wait_recv()
            for j in range(NCH):
                out = slice(j * CHUNK, (j + 1) * CHUNK)
                acc[:, out] += nt(xn[:, cols], rv[out, cols])

    gram = None
    for c in range(NCH):
        cols = slice(c * CHUNK, (c + 1) * CHUNK)

        @pl.when(me > 0)
        def _():
            c_copy(c).wait_recv()
            acc[:, cols] += cr[:, cols].astype(F32)

        y = acc[:, cols].astype(BF16)
        y_out[:, cols] = y
        g = nt(y, y)
        gram = g if gram is None else gram + g
    full[0:C, 0:C] = gram
    pack_symmetric(full, part)
    finish = exchange_sum(me, sector, count, part, recv, total, (s1, s2, s3, s4), 1.0 / (count * ROWS))

    for c in range(NCH):
        @pl.when(me > 0)
        def _():
            x_copy(c).wait_send()

        @pl.when(me < count - 1)
        def _():
            c_copy(c).wait_send()

    finish()
    b00, b01, b11, b02, b12, b22 = unpack_upper(total)
    s_out[...] = jnp.zeros((3, N, BLOCK), F32)
    s_out[0, 0:128, :] = b00
    s_out[1, 0:128, :] = b01
    s_out[2, 0:128, :] = b02
    s_out[1, 128:256, :] = b11
    s_out[2, 128:256, :] = b12
    extra = (iota((48, 128), 0) == iota((48, 128), 1)) & (iota((48, 128), 0) >= 44)
    s_out[2, 256:304, :] = jnp.where(extra, 1.0, b22)


def front(count, pattern, x, d, r):
    dma = pltpu.SemaphoreType.DMA
    return pl.pallas_call(
        lambda *refs: front_kernel(count, *refs),
        out_shape=(jax.ShapeDtypeStruct((C, ROWS), BF16), jax.ShapeDtypeStruct((3, N, BLOCK), F32)),
        in_specs=[pl.BlockSpec(memory_space=pltpu.SMEM)] + [pl.BlockSpec(memory_space=pl.ANY)] * 3,
        out_specs=(pl.BlockSpec(memory_space=pltpu.VMEM),) * 2,
        scratch_shapes=[
            pltpu.VMEM((C, ROWS), BF16), pltpu.VMEM((C, ROWS), BF16),
            pltpu.VMEM((ROWS, ROWS), BF16), pltpu.VMEM((ROWS, ROWS), BF16),
            pltpu.VMEM((C, ROWS), F32), pltpu.VMEM((C, ROWS), BF16), pltpu.VMEM((C, ROWS), BF16),
            pltpu.VMEM((N, LANES), F32), pltpu.VMEM((512, BLOCK), F32),
            pltpu.VMEM((count, 512 // count, BLOCK), F32), pltpu.VMEM((512, BLOCK), F32),
            dma((1 + 2 * NCH,)), dma((NCH,)), dma((NCH,)), dma((NCH,)), dma((NCH,)),
            dma((count,)), dma((count,)), dma((count,)), dma((count,)),
        ],
        compiler_params=pltpu.CompilerParams(collective_id=0, has_side_effects=True, vmem_limit_bytes=60 << 20),
        name="front",
    )(pattern, x, d, r)


def factor_kernel(s_ref, o_ref, w):
    w[...] = s_ref[...]
    chol_body(w)
    for t in range(3):
        keep = iota((N, BLOCK), 1) + BLOCK * t <= iota((N, BLOCK), 0)
        o_ref[:, BLOCK * t:BLOCK * (t + 1)] = jnp.where(keep, w[t], 0.0)


def factor(s):
    vmem = pl.BlockSpec(memory_space=pltpu.VMEM)
    return pl.pallas_call(
        factor_kernel, out_shape=jax.ShapeDtypeStruct((N, LANES), F32), in_specs=[vmem], out_specs=vmem,
        scratch_shapes=[pltpu.VMEM((3, N, BLOCK), F32)],
        compiler_params=pltpu.CompilerParams(vmem_limit_bytes=16 << 20), name="factor",
        cost_estimate=pl.CostEstimate(flops=10**10, bytes_accessed=10**6, transcendentals=0),
    )(s)


SYM = 512
CROSS = 768


def split(value):
    high = value.astype(BF16)
    return high, (value - high.astype(F32)).astype(BF16)


def tail_kernel(count, sectors, x, y, yp, linv, q_out, h_out, c_out,
                full, part, recv, total, linvp, lsend, lrecv, s1, s2, s3, s4):
    me = lax.axis_index("rows")
    sector = lax.axis_index("sector")
    linvp[...] = jnp.zeros((N, LANES), F32)
    barrier = greet(me, sector, count)

    @pl.when(sector > 0)
    def _():
        pl.semaphore_signal(barrier, inc=1, device_id=(sector - 1, me), device_id_type=MESH)

    @pl.when(sector < sectors - 1)
    def _():
        pl.semaphore_signal(barrier, inc=1, device_id=(sector + 1, me), device_id_type=MESH)

    full[...] = jnp.zeros((N, LANES), F32)
    full[0:C, 0:C] = nt(x[...], y[...])
    pack_symmetric(full, part)
    full[0:C, 0:C] = nt(yp[...], y[...])
    part[SYM:SYM + N, :] = full[:, 0:128]
    part[SYM + N:SYM + 2 * N, :] = full[:, 128:256]
    part[SYM + 2 * N:SYM + 2 * N + 152, :] = full[0:152, 256:384] + pltpu.roll(full[152:304, 256:384], 64, 1)
    part[SYM + 2 * N + 152:SYM + CROSS, :] = jnp.zeros((8, BLOCK), F32)

    both = jnp.where((sector > 0) & (sector < sectors - 1), 2, 1)
    pl.semaphore_wait(barrier, count - 1 + both)

    def l_copy(b, start, stop):
        piece = (pl.ds(start, stop - start), pl.ds(0, BLOCK * (b + 1)))
        return pltpu.make_async_remote_copy(
            src_ref=linv.at[piece], dst_ref=linvp.at[piece], send_sem=lsend.at[b], recv_sem=lrecv.at[b],
            device_id=(sector + 1, me), device_id_type=MESH)

    spans = ((0, 0, 128), (1, 128, 256), (2, 256, 304))

    @pl.when(sector < sectors - 1)
    def _():
        for span in spans:
            l_copy(*span).start()

    finish = exchange_sum(me, sector, count, part, recv, total, (s1, s2, s3, s4), 1.0 / (count * ROWS))
    high, low = split(linv[...])
    for c in range(NCH):
        cols = slice(c * CHUNK, (c + 1) * CHUNK)
        block = y[:, cols]
        q_out[:, cols] = (nn(high[0:C, 0:C], block) + nn(low[0:C, 0:C], block)).astype(BF16)
    finish()
    b00, b01, b11, b02, b12, b22 = unpack_upper(total)
    h_out[0:128, 0:128] = b00
    h_out[0:128, 128:256] = b01
    h_out[0:128, 256:C] = b02[:, 0:44]
    h_out[128:256, 0:128] = b01.T
    h_out[128:256, 128:256] = b11
    h_out[128:256, 256:C] = b12[:, 0:44]
    h_out[256:C, 0:128] = b02.T[0:44]
    h_out[256:C, 128:256] = b12.T[0:44]
    h_out[256:C, 256:C] = b22[0:44, 0:44]
    full[:, 0:128] = total[SYM:SYM + N, :]
    full[:, 128:256] = total[SYM + N:SYM + 2 * N, :]
    last = total[SYM + 2 * N:SYM + 2 * N + 152, :]
    left = iota((152, BLOCK), 1) < 64
    full[0:152, 256:384] = jnp.where(left, last, 0.0)
    full[152:304, 256:384] = jnp.where(left, pltpu.roll(last, 64, 1), 0.0)
    right = nt(full[...], linv[...], HI)

    @pl.when(sector > 0)
    def _():
        for span in spans:
            l_copy(*span).wait_recv()

    c_out[...] = nn(linvp[:, 0:N], right, HI)[0:C, 0:C]

    @pl.when(sector < sectors - 1)
    def _():
        for span in spans:
            l_copy(*span).wait_send()


def tail(count, sectors, x, y, yp, linv):
    dma = pltpu.SemaphoreType.DMA
    vmem = pl.BlockSpec(memory_space=pltpu.VMEM)
    size = SYM + CROSS
    return pl.pallas_call(
        lambda *refs: tail_kernel(count, sectors, *refs),
        out_shape=(jax.ShapeDtypeStruct((C, ROWS), BF16), jax.ShapeDtypeStruct((C, C), F32),
                   jax.ShapeDtypeStruct((C, C), F32)),
        in_specs=[vmem] * 4, out_specs=(vmem,) * 3,
        scratch_shapes=[
            pltpu.VMEM((N, LANES), F32), pltpu.VMEM((size, BLOCK), F32),
            pltpu.VMEM((count, size // count, BLOCK), F32), pltpu.VMEM((size, BLOCK), F32),
            pltpu.VMEM((N, LANES), F32), dma((3,)), dma((3,)),
            dma((count,)), dma((count,)), dma((count,)), dma((count,)),
        ],
        compiler_params=pltpu.CompilerParams(collective_id=1, has_side_effects=True, vmem_limit_bytes=40 << 20),
        name="tail",
    )(x, y, yp, linv)


def shards(x_block, h_diag, h_right, pattern):
    count, sectors = lax.axis_size("rows"), lax.axis_size("sector")
    x = x_block[0].T
    y, s = front(count, jnp.swapaxes(pattern[0], 0, 1), x, h_diag[0], h_right[0])
    yp = lax.ppermute(y, "sector", [(i, i + 1) for i in range(sectors - 1)])
    linv = factor(s)
    q, h, corr = tail(count, sectors, x, y, yp, linv)
    return q.T[None], h[None], corr[None]


def solution(mesh):
    in_specs = (
        P("sector", "rows", None),
        P("sector", "rows", None),
        P("sector", "rows", None),
        P("sector", None, "rows", None),
    )
    out_specs = (P("sector", "rows", None), P("sector", None, None), P("sector", None, None))
    return jax.shard_map(shards, mesh=mesh, in_specs=in_specs, out_specs=out_specs, check_vma=False)
```

```python
import jax
import jax.numpy as jnp
from jax import lax
from jax.experimental import pallas as pl
from jax.experimental.pallas import tpu as pltpu
from jax.sharding import PartitionSpec as P

HI = lax.Precision.HIGHEST
MESH = pl.DeviceIdType.MESH
F32 = jnp.float32
BF16 = jnp.bfloat16
N = 304
LANES = 384
C = 300
ROWS = 1280
CHUNK = 256
NCH = ROWS // CHUNK
BLOCK = 128


def nt(a, b, precision=None):
    return lax.dot_general(a, b, (((1,), (1,)), ((), ())), precision=precision, preferred_element_type=F32)


def tn(a, b, precision=None):
    return lax.dot_general(a, b, (((0,), (0,)), ((), ())), precision=precision, preferred_element_type=F32)


def nn(a, b, precision=None):
    return lax.dot_general(a, b, (((1,), (0,)), ((), ())), precision=precision, preferred_element_type=F32)


def panel_block(tiles, base_lane, count):
    lane = lax.broadcasted_iota(jnp.int32, (8, 128), 1)
    sub = lax.broadcasted_iota(jnp.int32, (8, 128), 0)
    ntile = len(tiles[0])
    for k in range(count):
        lo = 8 * k
        inside = (lane >= lo) & (lane < lo + 8)
        P = tiles[k]
        rows = [[jnp.broadcast_to(P[t][q:q + 1, :], (8, 128)) for t in range(ntile)] for q in range(8)]
        s = [[jnp.broadcast_to(rows[q][0][:, lo + p:lo + p + 1], (8, 128)) if p >= q else None for p in range(8)] for q in range(8)]
        for q in range(8):
            rows[q][0] = jnp.where(inside, jnp.where(lane == lo + q, 1.0, 0.0), rows[q][0])
        u = [[None] * 8 for _ in range(8)]
        rs = [None] * 8
        for p in range(8):
            rs[p] = lax.rsqrt(s[p][p])
            for r in range(p + 1, 8):
                u[p][r] = s[p][r] * rs[p]
            for q in range(p + 1, 8):
                for r in range(q, 8):
                    s[q][r] = s[q][r] - u[p][q] * u[p][r]
            rows[p] = [x * rs[p] for x in rows[p]]
            for q in range(p + 1, 8):
                rows[q] = [x - u[p][q] * y for x, y in zip(rows[q], rows[p])]
        fin = []
        for t in range(ntile):
            acc = rows[0][t]
            for q in range(1, 8):
                acc = jnp.where(sub == q, rows[q][t], acc)
            fin.append(acc)
        tiles[k] = fin
        for g in range(k + 1, count):
            cols = []
            for p in range(8):
                c = jnp.broadcast_to(tiles[g][0][:, lo + p:lo + p + 1], (8, 128))
                for q in range(p):
                    c = c - cols[q] * u[q][p]
                cols.append(c * rs[p])
            new = list(tiles[g])
            new[0] = jnp.where(inside, 0.0, new[0])
            for t in range(ntile):
                acc = new[t]
                for p in range(8):
                    acc = acc - cols[p] * rows[p][t]
                new[t] = acc
            tiles[g] = new
    return tiles


def iota(shape, dim):
    return lax.broadcasted_iota(jnp.int32, shape, dim)


def pack_symmetric(full, out):
    corner = pltpu.roll(full[256:304, 256:384], 0, 1)
    out[0:80, :] = full[0:80, 0:128]
    low = full[80:128, 0:128]
    out[80:128, :] = jnp.where(iota((48, 128), 1) < 48, corner, low)
    out[128:256, :] = full[0:128, 128:256]
    out[256:384, :] = full[128:256, 128:256]
    out[384:512, :] = full[0:128, 256:384] + pltpu.roll(full[128:256, 256:384], 64, 1)


def unpack_upper(packed):
    top = packed[0:128, :]
    upper = iota((128, 128), 1) >= iota((128, 128), 0)
    b00 = jnp.where(upper, top, top.T)
    b22 = jnp.where(iota((48, 128), 1) < 44, top[80:128, :], 0.0)
    both = packed[384:512, :]
    left = iota((128, 128), 1) < 64
    b02 = jnp.where(left, both, 0.0)
    b12 = jnp.where(left, pltpu.roll(both, 64, 1), 0.0)
    return b00, packed[128:256, :], packed[256:384, :], b02, b12, b22


def split(value):
    high = value.astype(BF16)
    return high, (value - high.astype(F32)).astype(BF16)


def factor_block(w, b, count):
    r0 = BLOCK * b
    order = [b] + [t for t in range(3) if t != b]
    tiles = [[w[t, r0 + 8 * g:r0 + 8 * g + 8, :] for t in order] for g in range(count)]
    tiles = panel_block(tiles, r0, count)
    for g in range(count):
        for i, t in enumerate(order):
            w[t, r0 + 8 * g:r0 + 8 * g + 8, :] = tiles[g][i]


def later_rows(w, b):
    r0, r1 = BLOCK * b, BLOCK * (b + 1)
    left = jnp.concatenate([w[t, r0:r1, :] for t in range(b + 1, 3)], axis=1)
    for t in range(3):
        right = w[t, r0:r1, :]
        if t == b:
            right = jnp.where(iota((BLOCK, BLOCK), 1) <= iota((BLOCK, BLOCK), 0), right, 0.0)
        update = tn(left, right, HI)[:N - r1]
        w[t, r1:N, :] = -update if t == b else w[t, r1:N, :] - update


class Sum:
    def __init__(self, me, sector, count, part, recv, total, sems, scale):
        self.me, self.sector, self.count = me, sector, count
        self.part, self.recv, self.total, self.sems, self.scale = part, recv, total, sems, scale
        self.size = part.shape[0] // count

    def rows_of(self, index):
        return pl.ds(pl.multiple_of(index * self.size, 8), self.size)

    def first(self, k):
        peer = lax.rem(self.me + k, self.count)
        return pltpu.make_async_remote_copy(
            src_ref=self.part.at[self.rows_of(peer)], dst_ref=self.recv.at[k],
            send_sem=self.sems[0].at[k], recv_sem=self.sems[1].at[k],
            device_id=(self.sector, peer), device_id_type=MESH)

    def second(self, k):
        peer = lax.rem(self.me + k, self.count)
        mine = self.total.at[self.rows_of(self.me)]
        return pltpu.make_async_remote_copy(
            src_ref=mine, dst_ref=mine, send_sem=self.sems[2].at[k], recv_sem=self.sems[3].at[k],
            device_id=(self.sector, peer), device_id_type=MESH)

    def each(self, action):
        def body(k, carry):
            action(k)
            return carry

        lax.fori_loop(1, self.count, body, 0)

    def scatter(self):
        self.each(lambda k: self.first(k).start())

    def gather(self):
        def add(k, acc):
            self.first(k).wait_recv()
            return acc + self.recv[k]

        acc = lax.fori_loop(1, self.count, add, self.part[self.rows_of(self.me), :])
        self.total[self.rows_of(self.me), :] = acc * self.scale
        self.each(lambda k: self.second(k).start())

    def finish(self):
        self.each(lambda k: self.second(k).wait_recv())

    def drain(self):
        def body(k):
            self.first(k).wait_send()
            self.second(k).wait_send()

        self.each(body)


SYM = 512
CROSS = 768
SPANS = ((0, 0, 128), (1, 128, 256), (2, 256, 304))


def kernel(count, sectors, pattern, x_hbm, d_hbm, r_hbm, q_out, h_out, c_out,
           xv, xn, dv, rv, acc, cs, cr, yv, yp, full, part, recv, total, part2, recv2, total2, w, linv, linvp,
           load, xsend, xrecv, csend, crecv, zsend, zrecv, lsend, lrecv, a1, a2, a3, a4, b1, b2, b3, b4):
    me = lax.axis_index("rows")
    sector = lax.axis_index("sector")
    has_next, has_last = me < count - 1, me > 0
    has_up, has_down = sector < sectors - 1, sector > 0
    columns = [slice(c * CHUNK, (c + 1) * CHUNK) for c in range(NCH)]

    loads = [pltpu.make_async_copy(x_hbm, xv, load.at[0])]
    for i, (source, target) in enumerate(((r_hbm, rv), (d_hbm, dv))):
        for c in range(NCH):
            cols = pl.ds(c * CHUNK, CHUNK)
            loads.append(pltpu.make_async_copy(source.at[:, cols], target.at[:, cols], load.at[1 + i * NCH + c]))
    for l in loads:
        l.start()
    linvp[...] = jnp.zeros((N, LANES), F32)

    barrier = pltpu.get_barrier_semaphore()

    def signal(k, carry):
        pl.semaphore_signal(barrier, inc=1, device_id=(sector, lax.rem(me + k, count)), device_id_type=MESH)
        return carry

    lax.fori_loop(1, count, signal, 0)

    @pl.when(has_down)
    def _():
        pl.semaphore_signal(barrier, inc=1, device_id=(sector - 1, me), device_id_type=MESH)

    @pl.when(has_up)
    def _():
        pl.semaphore_signal(barrier, inc=1, device_id=(sector + 1, me), device_id_type=MESH)

    both = jnp.where(has_down & has_up, 2, 1)
    pl.semaphore_wait(barrier, count - 1 + both)

    def remote(source, target, send, arrive, c, device):
        cols = pl.ds(c * CHUNK, CHUNK)
        return pltpu.make_async_remote_copy(
            src_ref=source.at[:, cols], dst_ref=target.at[:, cols], send_sem=send.at[c], recv_sem=arrive.at[c],
            device_id=device, device_id_type=MESH)

    def x_copy(c):
        return remote(x_hbm, xn, xsend, xrecv, c, (sector, me - 1))

    def c_copy(c):
        return remote(cs, cr, csend, crecv, c, (sector, me + 1))

    def z_copy(c):
        return remote(yv, yp, zsend, zrecv, c, (sector + 1, me))

    def l_copy(b, start, stop):
        piece = (pl.ds(start, stop - start), pl.ds(0, BLOCK * (b + 1)))
        return pltpu.make_async_remote_copy(
            src_ref=linv.at[piece], dst_ref=linvp.at[piece], send_sem=lsend.at[b], recv_sem=lrecv.at[b],
            device_id=(sector + 1, me), device_id_type=MESH)

    @pl.when(has_last)
    def _():
        for c in range(NCH):
            x_copy(c).start()

    full[...] = jnp.zeros((N, LANES), F32)

    @pl.when(sector == 0)
    def _():
        yp[...] = jnp.zeros((C, ROWS), BF16)

    def mask(tile, which, c):
        for i in range(ROWS // BLOCK):
            for j in range(CHUNK // BLOCK):
                row = slice(i * BLOCK, (i + 1) * BLOCK)
                col = slice(c * CHUNK + j * BLOCK, c * CHUNK + (j + 1) * BLOCK)
                keep = pattern[i, which, c * (CHUNK // BLOCK) + j]
                scale = jnp.full((BLOCK, BLOCK), keep.astype(F32)).astype(BF16)
                tile[row, col] = tile[row, col] * scale

    loads[0].wait()
    for c, cols in enumerate(columns):
        loads[1 + c].wait()
        mask(rv, 1, c)
        cs[:, cols] = nn(xv[...], rv[:, cols]).astype(BF16)

        @pl.when(has_next)
        def _():
            c_copy(c).start()

    for c, cols in enumerate(columns):
        loads[1 + NCH + c].wait()
        mask(dv, 0, c)
        acc[:, cols] = nn(xv[...], dv[:, cols])

    for c, cols in enumerate(columns):
        @pl.when(has_next)
        def _():
            x_copy(c).wait_recv()
            for out in columns:
                acc[:, out] += nt(xn[:, cols], rv[out, cols])

    gram = None
    for c, cols in enumerate(columns):
        @pl.when(has_last)
        def _():
            c_copy(c).wait_recv()
            acc[:, cols] += cr[:, cols].astype(F32)

        y = acc[:, cols].astype(BF16)
        yv[:, cols] = y

        @pl.when(has_up)
        def _():
            z_copy(c).start()

        g = nt(y, y)
        gram = g if gram is None else gram + g

    scale = 1.0 / (count * ROWS)
    full[0:C, 0:C] = gram
    pack_symmetric(full, part)
    gram_sum = Sum(me, sector, count, part, recv, total, (a1, a2, a3, a4), scale)
    gram_sum.scatter()
    full[0:C, 0:C] = nt(xv[...], yv[...])
    pack_symmetric(full, part2)
    gram_sum.gather()

    cross = None
    for c, cols in enumerate(columns):
        @pl.when(has_down)
        def _():
            z_copy(c).wait_recv()

        g = nt(yp[:, cols], yv[:, cols])
        cross = g if cross is None else cross + g
    full[0:C, 0:C] = cross
    part2[SYM:SYM + N, :] = full[:, 0:128]
    part2[SYM + N:SYM + 2 * N, :] = full[:, 128:256]
    part2[SYM + 2 * N:SYM + 2 * N + 152, :] = full[0:152, 256:384] + pltpu.roll(full[152:304, 256:384], 64, 1)
    part2[SYM + 2 * N + 152:SYM + CROSS, :] = jnp.zeros((8, BLOCK), F32)
    other_sum = Sum(me, sector, count, part2, recv2, total2, (b1, b2, b3, b4), scale)
    other_sum.scatter()

    gram_sum.finish()
    b00, b01, b11, b02, b12, b22 = unpack_upper(total)
    w[...] = jnp.zeros((3, N, BLOCK), F32)
    w[0, 0:128, :] = b00
    w[1, 0:128, :] = b01
    w[2, 0:128, :] = b02
    w[1, 128:256, :] = b11
    w[2, 128:256, :] = b12
    extra = (iota((48, 128), 0) == iota((48, 128), 1)) & (iota((48, 128), 0) >= 44)
    w[2, 256:304, :] = jnp.where(extra, 1.0, b22)

    for b, start, stop in SPANS:
        factor_block(w, b, (stop - start) // 8)
        if b < 2:
            later_rows(w, b)
        for t in range(3):
            shape = (stop - start, BLOCK)
            keep = iota(shape, 1) + BLOCK * t <= iota(shape, 0) + start
            linv[start:stop, BLOCK * t:BLOCK * (t + 1)] = jnp.where(keep, w[t, start:stop, :], 0.0)

        @pl.when(has_up)
        def _():
            l_copy(b, start, stop).start()

        if b == 0:
            other_sum.gather()

    high, low = split(linv[...])
    for cols in columns:
        block = yv[:, cols]
        q_out[:, cols] = (nn(high[0:C, 0:C], block) + nn(low[0:C, 0:C], block)).astype(BF16)

    other_sum.finish()
    b00, b01, b11, b02, b12, b22 = unpack_upper(total2)
    h_out[0:128, 0:128] = b00
    h_out[0:128, 128:256] = b01
    h_out[0:128, 256:C] = b02[:, 0:44]
    h_out[128:256, 0:128] = b01.T
    h_out[128:256, 128:256] = b11
    h_out[128:256, 256:C] = b12[:, 0:44]
    h_out[256:C, 0:128] = b02.T[0:44]
    h_out[256:C, 128:256] = b12.T[0:44]
    h_out[256:C, 256:C] = b22[0:44, 0:44]
    full[:, 0:128] = total2[SYM:SYM + N, :]
    full[:, 128:256] = total2[SYM + N:SYM + 2 * N, :]
    last = total2[SYM + 2 * N:SYM + 2 * N + 152, :]
    left = iota((152, BLOCK), 1) < 64
    full[0:152, 256:384] = jnp.where(left, last, 0.0)
    full[152:304, 256:384] = jnp.where(left, pltpu.roll(last, 64, 1), 0.0)
    right = nt(full[...], linv[...], HI)

    @pl.when(has_down)
    def _():
        for span in SPANS:
            l_copy(*span).wait_recv()

    c_out[...] = nn(linvp[:, 0:N], right, HI)[0:C, 0:C]

    for c in range(NCH):
        @pl.when(has_last)
        def _():
            x_copy(c).wait_send()

        @pl.when(has_next)
        def _():
            c_copy(c).wait_send()

        @pl.when(has_up)
        def _():
            z_copy(c).wait_send()

    @pl.when(has_up)
    def _():
        for span in SPANS:
            l_copy(*span).wait_send()

    gram_sum.drain()
    other_sum.drain()


def shards(x_block, h_diag, h_right, pattern):
    count, sectors = lax.axis_size("rows"), lax.axis_size("sector")
    dma = pltpu.SemaphoreType.DMA
    vmem = pl.BlockSpec(memory_space=pltpu.VMEM)
    rows_b, square, size = (C, ROWS), (ROWS, ROWS), SYM + CROSS
    q, h, corr = pl.pallas_call(
        lambda *refs: kernel(count, sectors, *refs),
        out_shape=(jax.ShapeDtypeStruct((C, ROWS), BF16), jax.ShapeDtypeStruct((C, C), F32),
                   jax.ShapeDtypeStruct((C, C), F32)),
        in_specs=[pl.BlockSpec(memory_space=pltpu.SMEM)] + [pl.BlockSpec(memory_space=pl.ANY)] * 3,
        out_specs=(vmem,) * 3,
        scratch_shapes=[
            pltpu.VMEM(rows_b, BF16), pltpu.VMEM(rows_b, BF16), pltpu.VMEM(square, BF16), pltpu.VMEM(square, BF16),
            pltpu.VMEM(rows_b, F32), pltpu.VMEM(rows_b, BF16), pltpu.VMEM(rows_b, BF16), pltpu.VMEM(rows_b, BF16),
            pltpu.VMEM(rows_b, BF16), pltpu.VMEM((N, LANES), F32),
            pltpu.VMEM((SYM, BLOCK), F32), pltpu.VMEM((count, SYM // count, BLOCK), F32), pltpu.VMEM((SYM, BLOCK), F32),
            pltpu.VMEM((size, BLOCK), F32), pltpu.VMEM((count, size // count, BLOCK), F32),
            pltpu.VMEM((size, BLOCK), F32),
            pltpu.VMEM((3, N, BLOCK), F32), pltpu.VMEM((N, LANES), F32), pltpu.VMEM((N, LANES), F32),
            dma((1 + 2 * NCH,)), dma((NCH,)), dma((NCH,)), dma((NCH,)), dma((NCH,)), dma((NCH,)), dma((NCH,)),
            dma((3,)), dma((3,)),
        ] + [dma((count,))] * 8,
        compiler_params=pltpu.CompilerParams(collective_id=0, has_side_effects=True, vmem_limit_bytes=60 << 20),
        name="step",
    )(jnp.swapaxes(pattern[0], 0, 1), x_block[0].T, h_diag[0], h_right[0])
    return q.T[None], h[None], corr[None]


def solution(mesh):
    in_specs = (
        P("sector", "rows", None),
        P("sector", "rows", None),
        P("sector", "rows", None),
        P("sector", None, "rows", None),
    )
    out_specs = (P("sector", "rows", None), P("sector", None, None), P("sector", None, None))
    return jax.shard_map(shards, mesh=mesh, in_specs=in_specs, out_specs=out_specs, check_vma=False)
```

```python
import jax
import jax.numpy as jnp
from jax import lax
from jax.experimental import pallas as pl
from jax.experimental.pallas import tpu as pltpu
from jax.sharding import PartitionSpec as P

HI = lax.Precision.HIGHEST
MESH = pl.DeviceIdType.MESH
F32 = jnp.float32
BF16 = jnp.bfloat16
N = 304
LANES = 384
C = 300
ROWS = 1280
CHUNK = 256
NCH = ROWS // CHUNK
BLOCK = 128


def nt(a, b, precision=None):
    return lax.dot_general(a, b, (((1,), (1,)), ((), ())), precision=precision, preferred_element_type=F32)


def tn(a, b, precision=None):
    return lax.dot_general(a, b, (((0,), (0,)), ((), ())), precision=precision, preferred_element_type=F32)


def nn(a, b, precision=None):
    return lax.dot_general(a, b, (((1,), (0,)), ((), ())), precision=precision, preferred_element_type=F32)


def panel_block(tiles, base_lane, count):
    lane = lax.broadcasted_iota(jnp.int32, (8, 128), 1)
    sub = lax.broadcasted_iota(jnp.int32, (8, 128), 0)
    ntile = len(tiles[0])
    for k in range(count):
        lo = 8 * k
        inside = (lane >= lo) & (lane < lo + 8)
        P = tiles[k]
        rows = [[jnp.broadcast_to(P[t][q:q + 1, :], (8, 128)) for t in range(ntile)] for q in range(8)]
        s = [[jnp.broadcast_to(rows[q][0][:, lo + p:lo + p + 1], (8, 128)) if p >= q else None for p in range(8)] for q in range(8)]
        for q in range(8):
            rows[q][0] = jnp.where(inside, jnp.where(lane == lo + q, 1.0, 0.0), rows[q][0])
        u = [[None] * 8 for _ in range(8)]
        rs = [None] * 8
        for p in range(8):
            rs[p] = lax.rsqrt(s[p][p])
            for r in range(p + 1, 8):
                u[p][r] = s[p][r] * rs[p]
            for q in range(p + 1, 8):
                for r in range(q, 8):
                    s[q][r] = s[q][r] - u[p][q] * u[p][r]
            rows[p] = [x * rs[p] for x in rows[p]]
            for q in range(p + 1, 8):
                rows[q] = [x - u[p][q] * y for x, y in zip(rows[q], rows[p])]
        fin = []
        for t in range(ntile):
            acc = rows[0][t]
            for q in range(1, 8):
                acc = jnp.where(sub == q, rows[q][t], acc)
            fin.append(acc)
        tiles[k] = fin
        for g in range(k + 1, count):
            cols = []
            for p in range(8):
                c = jnp.broadcast_to(tiles[g][0][:, lo + p:lo + p + 1], (8, 128))
                for q in range(p):
                    c = c - cols[q] * u[q][p]
                cols.append(c * rs[p])
            new = list(tiles[g])
            new[0] = jnp.where(inside, 0.0, new[0])
            for t in range(ntile):
                acc = new[t]
                for p in range(8):
                    acc = acc - cols[p] * rows[p][t]
                new[t] = acc
            tiles[g] = new
    return tiles


def iota(shape, dim):
    return lax.broadcasted_iota(jnp.int32, shape, dim)


def pack_symmetric(full, out):
    corner = pltpu.roll(full[256:304, 256:384], 0, 1)
    out[0:80, :] = full[0:80, 0:128]
    low = full[80:128, 0:128]
    out[80:128, :] = jnp.where(iota((48, 128), 1) < 48, corner, low)
    out[128:256, :] = full[0:128, 128:256]
    out[256:384, :] = full[128:256, 128:256]
    out[384:512, :] = full[0:128, 256:384] + pltpu.roll(full[128:256, 256:384], 64, 1)


def unpack_upper(packed):
    top = packed[0:128, :]
    upper = iota((128, 128), 1) >= iota((128, 128), 0)
    b00 = jnp.where(upper, top, top.T)
    b22 = jnp.where(iota((48, 128), 1) < 44, top[80:128, :], 0.0)
    both = packed[384:512, :]
    left = iota((128, 128), 1) < 64
    b02 = jnp.where(left, both, 0.0)
    b12 = jnp.where(left, pltpu.roll(both, 64, 1), 0.0)
    return b00, packed[128:256, :], packed[256:384, :], b02, b12, b22


def split(value):
    high = value.astype(BF16)
    return high, (value - high.astype(F32)).astype(BF16)


def factor_block(w, b, count):
    r0 = BLOCK * b
    order = [b] + [t for t in range(3) if t != b]
    tiles = [[w[t, r0 + 8 * g:r0 + 8 * g + 8, :] for t in order] for g in range(count)]
    tiles = panel_block(tiles, r0, count)
    for g in range(count):
        for i, t in enumerate(order):
            w[t, r0 + 8 * g:r0 + 8 * g + 8, :] = tiles[g][i]


def later_rows(w, b):
    r0, r1 = BLOCK * b, BLOCK * (b + 1)
    left = jnp.concatenate([w[t, r0:r1, :] for t in range(b + 1, 3)], axis=1)
    for t in range(3):
        right = w[t, r0:r1, :]
        if t == b:
            right = jnp.where(iota((BLOCK, BLOCK), 1) <= iota((BLOCK, BLOCK), 0), right, 0.0)
        update = tn(left, right, HI)[:N - r1]
        w[t, r1:N, :] = -update if t == b else w[t, r1:N, :] - update


class Sum:
    def __init__(self, me, sector, count, part, recv, total, sems, scale):
        self.me, self.sector, self.count = me, sector, count
        self.part, self.recv, self.total, self.sems, self.scale = part, recv, total, sems, scale
        self.size = part.shape[0] // count

    def rows_of(self, index):
        return pl.ds(pl.multiple_of(index * self.size, 8), self.size)

    def first(self, k):
        peer = lax.rem(self.me + k, self.count)
        return pltpu.make_async_remote_copy(
            src_ref=self.part.at[self.rows_of(peer)], dst_ref=self.recv.at[k],
            send_sem=self.sems[0].at[k], recv_sem=self.sems[1].at[k],
            device_id=(self.sector, peer), device_id_type=MESH)

    def second(self, k):
        peer = lax.rem(self.me + k, self.count)
        mine = self.total.at[self.rows_of(self.me)]
        return pltpu.make_async_remote_copy(
            src_ref=mine, dst_ref=mine, send_sem=self.sems[2].at[k], recv_sem=self.sems[3].at[k],
            device_id=(self.sector, peer), device_id_type=MESH)

    def each(self, action):
        def body(k, carry):
            action(k)
            return carry

        lax.fori_loop(1, self.count, body, 0)

    def scatter(self):
        self.each(lambda k: self.first(k).start())

    def gather(self):
        def add(k, acc):
            self.first(k).wait_recv()
            return acc + self.recv[k]

        acc = lax.fori_loop(1, self.count, add, self.part[self.rows_of(self.me), :])
        self.total[self.rows_of(self.me), :] = acc * self.scale
        self.each(lambda k: self.second(k).start())

    def finish(self):
        self.each(lambda k: self.second(k).wait_recv())

    def drain(self):
        def body(k):
            self.first(k).wait_send()
            self.second(k).wait_send()

        self.each(body)


SYM = 512
CROSS = 768
SPANS = ((0, 0, 128), (1, 128, 256), (2, 256, 304))


def kernel(count, sectors, pattern, x_hbm, d_hbm, r_hbm, q_out, sums_out, linv_out, linvp_out,
           xv, xn, dv, rv, acc, cs, cr, yv, yp, full, part, recv, total, part_h, recv_h, part_c, recv_c, total2, w, linv, linvp, qv,
           load, xsend, xrecv, csend, crecv, zsend, zrecv, lsend, lrecv, outsem, a1, a2, a3, a4, h1, h2, c1, c2, b1, b2):
    me = lax.axis_index("rows")
    sector = lax.axis_index("sector")
    has_next, has_last = me < count - 1, me > 0
    has_up, has_down = sector < sectors - 1, sector > 0
    core = lax.rem(me, 2)
    z_sends = ((core == 0) & has_up) | ((core == 1) & has_down)
    z_arrives = ((core == 0) & has_down) | ((core == 1) & has_up)
    columns = [slice(c * CHUNK, (c + 1) * CHUNK) for c in range(NCH)]

    loads = [pltpu.make_async_copy(x_hbm, xv, load.at[0])]
    for i, (source, target) in enumerate(((r_hbm, rv), (d_hbm, dv))):
        for c in range(NCH):
            cols = pl.ds(c * CHUNK, CHUNK)
            loads.append(pltpu.make_async_copy(source.at[:, cols], target.at[:, cols], load.at[1 + i * NCH + c]))
    for l in loads:
        l.start()
    linvp[...] = jnp.zeros((N, LANES), F32)

    barrier = pltpu.get_barrier_semaphore()

    def signal(k, carry):
        pl.semaphore_signal(barrier, inc=1, device_id=(sector, lax.rem(me + k, count)), device_id_type=MESH)
        return carry

    lax.fori_loop(1, count, signal, 0)

    @pl.when(has_down)
    def _():
        def signal_below(k, carry):
            pl.semaphore_signal(barrier, inc=1, device_id=(sector - 1, 2 * k + 1), device_id_type=MESH)
            return carry

        lax.fori_loop(0, count // 2, signal_below, 0)

    @pl.when(has_down & (core == 0))
    def _():
        pl.semaphore_signal(barrier, inc=1, device_id=(sector - 1, me), device_id_type=MESH)

    @pl.when(has_up & (core == 1))
    def _():
        pl.semaphore_signal(barrier, inc=1, device_id=(sector + 1, me), device_id_type=MESH)

    above = jnp.where(has_up, jnp.where(core == 1, count, 1), 0)
    below = jnp.where(has_down & (core == 1), 1, 0)
    pl.semaphore_wait(barrier, count - 1 + above + below)

    def remote(source, target, send, arrive, c, device):
        cols = pl.ds(c * CHUNK, CHUNK)
        return pltpu.make_async_remote_copy(
            src_ref=source.at[:, cols], dst_ref=target.at[:, cols], send_sem=send.at[c], recv_sem=arrive.at[c],
            device_id=device, device_id_type=MESH)

    def x_copy(c):
        return remote(x_hbm, xn, xsend, xrecv, c, (sector, me - 1))

    def c_copy(c):
        return remote(cs, cr, csend, crecv, c, (sector, me + 1))

    def z_copy(c):
        return remote(yv, yp, zsend, zrecv, c, (sector + 1 - 2 * core, me))

    def l_copy(b, start, stop):
        piece = (pl.ds(start, stop - start), pl.ds(0, BLOCK * (b + 1)))
        return pltpu.make_async_remote_copy(
            src_ref=linv.at[piece], dst_ref=linvp.at[piece], send_sem=lsend.at[b], recv_sem=lrecv.at[b],
            device_id=(sector + 1, me), device_id_type=MESH)

    @pl.when(has_last)
    def _():
        for c in range(NCH):
            x_copy(c).start()

    full[...] = jnp.zeros((N, LANES), F32)

    def mask(tile, which, c):
        for i in range(ROWS // BLOCK):
            for j in range(CHUNK // BLOCK):
                row = slice(i * BLOCK, (i + 1) * BLOCK)
                col = slice(c * CHUNK + j * BLOCK, c * CHUNK + (j + 1) * BLOCK)
                keep = pattern[i, which, c * (CHUNK // BLOCK) + j]
                scale = jnp.full((BLOCK, BLOCK), keep.astype(F32)).astype(BF16)
                tile[row, col] = tile[row, col] * scale

    loads[0].wait()
    for c, cols in enumerate(columns):
        loads[1 + c].wait()
        mask(rv, 1, c)
        cs[:, cols] = nn(xv[...], rv[:, cols]).astype(BF16)

        @pl.when(has_next)
        def _():
            c_copy(c).start()

    for c, cols in enumerate(columns):
        loads[1 + NCH + c].wait()
        mask(dv, 0, c)
        acc[:, cols] = nn(xv[...], dv[:, cols])

    for c, cols in enumerate(columns):
        @pl.when(has_next)
        def _():
            x_copy(c).wait_recv()
            for out in columns:
                acc[:, out] += nt(xn[:, cols], rv[out, cols])

    gram = None
    for c, cols in enumerate(columns):
        @pl.when(has_last)
        def _():
            c_copy(c).wait_recv()
            acc[:, cols] += cr[:, cols].astype(F32)

        y = acc[:, cols].astype(BF16)
        yv[:, cols] = y

        @pl.when(z_sends)
        def _():
            z_copy(c).start()

        g = nt(y, y)
        gram = g if gram is None else gram + g

    scale = 1.0 / (count * ROWS)
    full[0:C, 0:C] = gram
    pack_symmetric(full, part)
    gram_sum = Sum(me, sector, count, part, recv, total, (a1, a2, a3, a4), scale)
    gram_sum.scatter()
    full[0:C, 0:C] = nt(xv[...], yv[...])
    pack_symmetric(full, part_h)
    gram_sum.gather()

    def each(lower, action):
        def body(k, carry):
            action(k)
            return carry

        lax.fori_loop(lower, count, body, 0)

    size_h, size_c = SYM // count, CROSS // count

    def chunk(index, size):
        return pl.ds(pl.multiple_of(index * size, 8), size)

    def h_copy(k):
        peer = lax.rem(me + k, count)
        return pltpu.make_async_remote_copy(
            src_ref=part_h.at[chunk(peer, size_h)], dst_ref=recv_h.at[k], send_sem=h1.at[k], recv_sem=h2.at[k],
            device_id=(sector, peer), device_id_type=MESH)

    def cross_copy(k):
        peer = lax.rem(me + k, count)
        return pltpu.make_async_remote_copy(
            src_ref=part_c.at[chunk(peer, size_c)], dst_ref=recv_c.at[k], send_sem=c1.at[k], recv_sem=c2.at[k],
            device_id=(sector + core, peer), device_id_type=MESH)

    def all_copy(k):
        peer = lax.rem(me + k, count)
        return pltpu.make_async_remote_copy(
            src_ref=total2.at[me], dst_ref=total2.at[me], send_sem=b1.at[k], recv_sem=b2.at[k],
            device_id=(sector, peer), device_id_type=MESH)

    each(1, lambda k: h_copy(k).start())
    full[...] = jnp.zeros((N, LANES), F32)
    for c, cols in enumerate(columns):
        @pl.when(z_arrives)
        def _():
            z_copy(c).wait_recv()

        @pl.when(z_arrives & (core == 0))
        def _():
            full[0:C, 0:C] += nt(yp[:, cols], yv[:, cols])

        @pl.when(z_arrives & (core == 1))
        def _():
            full[0:C, 0:C] += nt(yv[:, cols], yp[:, cols])

    part_c[0:N, :] = full[:, 0:128]
    part_c[N:2 * N, :] = full[:, 128:256]
    part_c[2 * N:2 * N + 152, :] = full[0:152, 256:384] + pltpu.roll(full[152:304, 256:384], 64, 1)
    part_c[2 * N + 152:CROSS, :] = jnp.zeros((8, BLOCK), F32)

    @pl.when(z_arrives)
    def _():
        each(1 - core, lambda k: cross_copy(k).start())

    def gather_both():
        def add_h(k, value):
            h_copy(k).wait_recv()
            return value + recv_h[k]

        def add_c(k, value):
            cross_copy(k).wait_recv()
            return value + recv_c[k]

        total2[me, 0:size_h, :] = lax.fori_loop(1, count, add_h, part_h[chunk(me, size_h), :]) * scale
        total2[me, size_h:size_h + size_c, :] = jnp.zeros((size_c, BLOCK), F32)

        @pl.when(has_down)
        def _():
            own = jnp.where(core == 0, part_c[chunk(me, size_c), :], 0.0)
            total2[me, size_h:size_h + size_c, :] = lax.fori_loop(1 - core, count, add_c, own) * scale

        each(1, lambda k: all_copy(k).start())

    gram_sum.finish()
    b00, b01, b11, b02, b12, b22 = unpack_upper(total)
    w[...] = jnp.zeros((3, N, BLOCK), F32)
    w[0, 0:128, :] = b00
    w[1, 0:128, :] = b01
    w[2, 0:128, :] = b02
    w[1, 128:256, :] = b11
    w[2, 128:256, :] = b12
    extra = (iota((48, 128), 0) == iota((48, 128), 1)) & (iota((48, 128), 0) >= 44)
    w[2, 256:304, :] = jnp.where(extra, 1.0, b22)

    for b, start, stop in SPANS:
        factor_block(w, b, (stop - start) // 8)
        if b < 2:
            later_rows(w, b)
        for t in range(3):
            shape = (stop - start, BLOCK)
            keep = iota(shape, 1) + BLOCK * t <= iota(shape, 0) + start
            linv[start:stop, BLOCK * t:BLOCK * (t + 1)] = jnp.where(keep, w[t, start:stop, :], 0.0)

        @pl.when(has_up)
        def _():
            l_copy(b, start, stop).start()

        if b == 0:
            gather_both()

    outs = [pltpu.make_async_copy(linv, linv_out, outsem.at[NCH])]
    outs[0].start()
    high, low = split(linv[...])
    for c, cols in enumerate(columns):
        block = yv[:, cols]
        qv[:, cols] = (nn(high[0:C, 0:C], block) + nn(low[0:C, 0:C], block)).astype(BF16)
        piece = pl.ds(c * CHUNK, CHUNK)
        outs.append(pltpu.make_async_copy(qv.at[:, piece], q_out.at[:, piece], outsem.at[c]))
        outs[-1].start()

    @pl.when(has_down)
    def _():
        for span in SPANS:
            l_copy(*span).wait_recv()

    outs.append(pltpu.make_async_copy(linvp, linvp_out, outsem.at[NCH + 1]))
    outs[-1].start()
    each(1, lambda k: all_copy(k).wait_recv())
    outs.append(pltpu.make_async_copy(total2, sums_out, outsem.at[NCH + 2]))
    outs[-1].start()
    for copy in outs:
        copy.wait()

    for c in range(NCH):
        @pl.when(has_last)
        def _():
            x_copy(c).wait_send()

        @pl.when(has_next)
        def _():
            c_copy(c).wait_send()

        @pl.when(z_sends)
        def _():
            z_copy(c).wait_send()

    @pl.when(has_up)
    def _():
        for span in SPANS:
            l_copy(*span).wait_send()

    gram_sum.drain()

    def drain(k):
        h_copy(k).wait_send()
        all_copy(k).wait_send()

    each(1, drain)

    @pl.when(z_arrives)
    def _():
        each(1 - core, lambda k: cross_copy(k).wait_send())


def finish_kernel(q_in, sums_in, linv_in, linvp_in, q_out, h_out, c_out, sums, linv, linvp, full, q, sem):
    pairs = ((q_in, q), (sums_in, sums), (linv_in, linv), (linvp_in, linvp))
    copies = [pltpu.make_async_copy(*pair, sem.at[i]) for i, pair in enumerate(pairs)]
    for copy in copies:
        copy.start()
    copies[0].wait()
    q_copy = pltpu.make_async_copy(q, q_out, sem.at[4])
    q_copy.start()
    for copy in copies[1:]:
        copy.wait()
    count, size = sums.shape[0], SYM // sums.shape[0]
    cross = sums[:, size:, :].reshape(CROSS, BLOCK)
    full[:, 0:128] = cross[0:N]
    full[:, 128:256] = cross[N:2 * N]
    last = cross[2 * N:2 * N + 152]
    left = iota((152, BLOCK), 1) < 64
    full[0:152, 256:384] = jnp.where(left, last, 0.0)
    full[152:304, 256:384] = jnp.where(left, pltpu.roll(last, 64, 1), 0.0)
    right = nt(full[...], linv[...], HI)
    c_out[:, 0, :] = nn(linvp[:, 0:N], right, HI)[0:C, 0:C]
    b00, b01, b11, b02, b12, b22 = unpack_upper(sums[:, 0:size, :].reshape(SYM, BLOCK))
    full[0:128, 0:128] = b00
    full[0:128, 128:256] = b01
    full[0:128, 256:384] = b02
    full[128:256, 0:128] = b01.T
    full[128:256, 128:256] = b11
    full[128:256, 256:384] = b12
    full[256:304, 0:128] = b02.T[0:48]
    full[256:304, 128:256] = b12.T[0:48]
    full[256:304, 256:384] = b22
    h_out[:, 0, :] = full[0:C, 0:C]
    q_copy.wait()


def finish(q, sums, linv, linvp):
    vmem = pl.BlockSpec(memory_space=pltpu.VMEM)
    anywhere = pl.BlockSpec(memory_space=pl.ANY)
    square = jax.ShapeDtypeStruct((C, 1, C), F32)
    return pl.pallas_call(
        finish_kernel, out_shape=(jax.ShapeDtypeStruct((C, ROWS), BF16), square, square),
        in_specs=[anywhere] * 4, out_specs=(anywhere, vmem, vmem),
        scratch_shapes=[pltpu.VMEM(sums.shape, F32)] + [pltpu.VMEM((N, LANES), F32)] * 3
        + [pltpu.VMEM((C, ROWS), BF16), pltpu.SemaphoreType.DMA((5,))],
        compiler_params=pltpu.CompilerParams(vmem_limit_bytes=57 << 20), name="finish",
    )(q, sums, linv, linvp)


def shards(x_block, h_diag, h_right, pattern):
    count, sectors = lax.axis_size("rows"), lax.axis_size("sector")
    dma = pltpu.SemaphoreType.DMA
    vmem = pl.BlockSpec(memory_space=pltpu.VMEM)
    rows_b, square, size = (C, ROWS), (ROWS, ROWS), SYM + CROSS
    q, sums, linv, linvp = pl.pallas_call(
        lambda *refs: kernel(count, sectors, *refs),
        out_shape=(jax.ShapeDtypeStruct((C, ROWS), BF16), jax.ShapeDtypeStruct((count, size // count, BLOCK), F32),
                   jax.ShapeDtypeStruct((N, LANES), F32), jax.ShapeDtypeStruct((N, LANES), F32)),
        in_specs=[pl.BlockSpec(memory_space=pltpu.SMEM)] + [pl.BlockSpec(memory_space=pl.ANY)] * 3,
        out_specs=(pl.BlockSpec(memory_space=pl.ANY),) * 4,
        scratch_shapes=[
            pltpu.VMEM(rows_b, BF16), pltpu.VMEM(rows_b, BF16), pltpu.VMEM(square, BF16), pltpu.VMEM(square, BF16),
            pltpu.VMEM(rows_b, F32), pltpu.VMEM(rows_b, BF16), pltpu.VMEM(rows_b, BF16), pltpu.VMEM(rows_b, BF16),
            pltpu.VMEM(rows_b, BF16), pltpu.VMEM((N, LANES), F32),
            pltpu.VMEM((SYM, BLOCK), F32), pltpu.VMEM((count, SYM // count, BLOCK), F32), pltpu.VMEM((SYM, BLOCK), F32),
            pltpu.VMEM((SYM, BLOCK), F32), pltpu.VMEM((count, SYM // count, BLOCK), F32),
            pltpu.VMEM((CROSS, BLOCK), F32), pltpu.VMEM((count, CROSS // count, BLOCK), F32),
            pltpu.VMEM((count, size // count, BLOCK), F32),
            pltpu.VMEM((3, N, BLOCK), F32), pltpu.VMEM((N, LANES), F32), pltpu.VMEM((N, LANES), F32),
            pltpu.VMEM(rows_b, BF16),
            dma((1 + 2 * NCH,)), dma((NCH,)), dma((NCH,)), dma((NCH,)), dma((NCH,)), dma((NCH,)), dma((NCH,)),
            dma((3,)), dma((3,)), dma((NCH + 3,)),
        ] + [dma((count,))] * 10,
        compiler_params=pltpu.CompilerParams(collective_id=0, has_side_effects=True, vmem_limit_bytes=57 << 20),
        name="step",
    )(jnp.swapaxes(pattern[0], 0, 1), x_block[0].T, h_diag[0], h_right[0])
    q, h, corr = finish(q, sums, linv, linvp)
    return q.T[None], jnp.swapaxes(h, 0, 1), jnp.swapaxes(corr, 0, 1)


def solution(mesh):
    in_specs = (
        P("sector", "rows", None),
        P("sector", "rows", None),
        P("sector", "rows", None),
        P("sector", None, "rows", None),
    )
    out_specs = (P("sector", "rows", None), P("sector", None, None), P("sector", None, None))
    return jax.shard_map(shards, mesh=mesh, in_specs=in_specs, out_specs=out_specs, check_vma=False)
```

```python
import jax
import jax.numpy as jnp
from jax import lax
from jax.experimental import pallas as pl
from jax.experimental.pallas import tpu as pltpu
from jax.sharding import PartitionSpec as P

HI = lax.Precision.HIGHEST
MESH = pl.DeviceIdType.MESH
F32 = jnp.float32
BF16 = jnp.bfloat16
N = 304
LANES = 384
C = 300
ROWS = 1280
CHUNK = 256
NCH = ROWS // CHUNK
BLOCK = 128


def nt(a, b, precision=None):
    return lax.dot_general(a, b, (((1,), (1,)), ((), ())), precision=precision, preferred_element_type=F32)


def tn(a, b, precision=None):
    return lax.dot_general(a, b, (((0,), (0,)), ((), ())), precision=precision, preferred_element_type=F32)


def nn(a, b, precision=None):
    return lax.dot_general(a, b, (((1,), (0,)), ((), ())), precision=precision, preferred_element_type=F32)


def panel_block(tiles, base_lane, count):
    lane = lax.broadcasted_iota(jnp.int32, (8, 128), 1)
    sub = lax.broadcasted_iota(jnp.int32, (8, 128), 0)
    ntile = len(tiles[0])
    for k in range(count):
        lo = 8 * k
        inside = (lane >= lo) & (lane < lo + 8)
        P = tiles[k]
        rows = [[jnp.broadcast_to(P[t][q:q + 1, :], (8, 128)) for t in range(ntile)] for q in range(8)]
        s = [[jnp.broadcast_to(rows[q][0][:, lo + p:lo + p + 1], (8, 128)) if p >= q else None for p in range(8)] for q in range(8)]
        for q in range(8):
            rows[q][0] = jnp.where(inside, jnp.where(lane == lo + q, 1.0, 0.0), rows[q][0])
        u = [[None] * 8 for _ in range(8)]
        rs = [None] * 8
        for p in range(8):
            rs[p] = lax.rsqrt(s[p][p])
            for r in range(p + 1, 8):
                u[p][r] = s[p][r] * rs[p]
            for q in range(p + 1, 8):
                for r in range(q, 8):
                    s[q][r] = s[q][r] - u[p][q] * u[p][r]
            rows[p] = [x * rs[p] for x in rows[p]]
            for q in range(p + 1, 8):
                rows[q] = [x - u[p][q] * y for x, y in zip(rows[q], rows[p])]
        fin = []
        for t in range(ntile):
            acc = rows[0][t]
            for q in range(1, 8):
                acc = jnp.where(sub == q, rows[q][t], acc)
            fin.append(acc)
        tiles[k] = fin
        for g in range(k + 1, count):
            cols = []
            for p in range(8):
                c = jnp.broadcast_to(tiles[g][0][:, lo + p:lo + p + 1], (8, 128))
                for q in range(p):
                    c = c - cols[q] * u[q][p]
                cols.append(c * rs[p])
            new = list(tiles[g])
            new[0] = jnp.where(inside, 0.0, new[0])
            for t in range(ntile):
                acc = new[t]
                for p in range(8):
                    acc = acc - cols[p] * rows[p][t]
                new[t] = acc
            tiles[g] = new
    return tiles


def iota(shape, dim):
    return lax.broadcasted_iota(jnp.int32, shape, dim)


def pack_symmetric(full, out):
    corner = pltpu.roll(full[256:304, 256:384], 0, 1)
    out[0:80, :] = full[0:80, 0:128]
    low = full[80:128, 0:128]
    out[80:128, :] = jnp.where(iota((48, 128), 1) < 48, corner, low)
    out[128:256, :] = full[0:128, 128:256]
    out[256:384, :] = full[128:256, 128:256]
    out[384:512, :] = full[0:128, 256:384] + pltpu.roll(full[128:256, 256:384], 64, 1)


def unpack_upper(packed):
    top = packed[0:128, :]
    upper = iota((128, 128), 1) >= iota((128, 128), 0)
    b00 = jnp.where(upper, top, top.T)
    b22 = jnp.where(iota((48, 128), 1) < 44, top[80:128, :], 0.0)
    both = packed[384:512, :]
    left = iota((128, 128), 1) < 64
    b02 = jnp.where(left, both, 0.0)
    b12 = jnp.where(left, pltpu.roll(both, 64, 1), 0.0)
    return b00, packed[128:256, :], packed[256:384, :], b02, b12, b22


def split(value):
    high = value.astype(BF16)
    return high, (value - high.astype(F32)).astype(BF16)


def factor_block(w, b, count):
    r0 = BLOCK * b
    order = [b] + [t for t in range(3) if t != b]
    tiles = [[w[t, r0 + 8 * g:r0 + 8 * g + 8, :] for t in order] for g in range(count)]
    tiles = panel_block(tiles, r0, count)
    for g in range(count):
        for i, t in enumerate(order):
            w[t, r0 + 8 * g:r0 + 8 * g + 8, :] = tiles[g][i]


def later_rows(w, b):
    r0, r1 = BLOCK * b, BLOCK * (b + 1)
    left = jnp.concatenate([w[t, r0:r1, :] for t in range(b + 1, 3)], axis=1)
    for t in range(3):
        right = w[t, r0:r1, :]
        if t == b:
            right = jnp.where(iota((BLOCK, BLOCK), 1) <= iota((BLOCK, BLOCK), 0), right, 0.0)
        update = tn(left, right, HI)[:N - r1]
        w[t, r1:N, :] = -update if t == b else w[t, r1:N, :] - update


def take(view, sem):
    pltpu.make_async_copy(view, view, sem).wait()


def each(lower, upper, action):
    def body(k, carry):
        action(k)
        return carry

    lax.fori_loop(lower, upper, body, 0)


SYM = 512
CROSS = 768
EARLY = 3
SPANS = ((0, 0, 128), (1, 128, 256), (2, 256, 304))


def kernel(count, sectors, pattern, x_hbm, d_hbm, r_hbm, q_out, sums_out, right_out, linvp_out,
           xv, xn, dv, rv, acc, cs, cr, yv, yp, full, part, recv, total, part_h, recv_h, part_c, recv_c, total2, w, linv, linvp, qv, right,
           load, xsend, xrecv, csend, crecv, zsend, zrecv, lsend, lrecv, outsem, a1, a2, a3, a4, h1, h2, c1, c2, b1, b2):
    me = lax.axis_index("rows")
    sector = lax.axis_index("sector")
    has_next, has_last = me < count - 1, me > 0
    has_up, has_down = sector < sectors - 1, sector > 0
    core = lax.rem(me, 2)
    z_sends = ((core == 0) & has_up) | ((core == 1) & has_down)
    z_arrives = ((core == 0) & has_down) | ((core == 1) & has_up)
    columns = [slice(c * CHUNK, (c + 1) * CHUNK) for c in range(NCH)]

    loads = [pltpu.make_async_copy(x_hbm, xv, load.at[0])]
    for i, (source, target) in enumerate(((r_hbm, rv), (d_hbm, dv))):
        for c in range(NCH):
            cols = pl.ds(c * CHUNK, CHUNK)
            loads.append(pltpu.make_async_copy(source.at[:, cols], target.at[:, cols], load.at[1 + i * NCH + c]))
    for l in loads:
        l.start()
    linvp[...] = jnp.zeros((N, LANES), F32)

    barrier = pltpu.get_barrier_semaphore()

    def signal(k, carry):
        pl.semaphore_signal(barrier, inc=1, device_id=(sector, lax.rem(me + k, count)), device_id_type=MESH)
        return carry

    lax.fori_loop(1, count, signal, 0)

    @pl.when(has_down)
    def _():
        def signal_below(k, carry):
            pl.semaphore_signal(barrier, inc=1, device_id=(sector - 1, 2 * k + 1), device_id_type=MESH)
            return carry

        lax.fori_loop(0, count // 2, signal_below, 0)

    @pl.when(has_down & (core == 0))
    def _():
        pl.semaphore_signal(barrier, inc=1, device_id=(sector - 1, me), device_id_type=MESH)

    @pl.when(has_up & (core == 1))
    def _():
        pl.semaphore_signal(barrier, inc=1, device_id=(sector + 1, me), device_id_type=MESH)

    above = jnp.where(has_up, jnp.where(core == 1, count, 1), 0)
    below = jnp.where(has_down & (core == 1), 1, 0)
    def mask(tile, which, c):
        for i in range(ROWS // BLOCK):
            for j in range(CHUNK // BLOCK):
                row = slice(i * BLOCK, (i + 1) * BLOCK)
                col = slice(c * CHUNK + j * BLOCK, c * CHUNK + (j + 1) * BLOCK)
                keep = pattern[i, which, c * (CHUNK // BLOCK) + j]
                scale = jnp.full((BLOCK, BLOCK), keep.astype(F32)).astype(BF16)
                tile[row, col] = tile[row, col] * scale

    def remote(source, target, send, arrive, c, device):
        cols = pl.ds(c * CHUNK, CHUNK)
        return pltpu.make_async_remote_copy(
            src_ref=source.at[:, cols], dst_ref=target.at[:, cols], send_sem=send.at[c], recv_sem=arrive.at[c],
            device_id=device, device_id_type=MESH)

    def x_copy(c):
        return remote(x_hbm, xn, xsend, xrecv, c, (sector, me - 1))

    def c_copy(c):
        return remote(cs, cr, csend, crecv, c, (sector, me + 1))

    def z_copy(c):
        return remote(yv, yp, zsend, zrecv, c, (sector + 1 - 2 * core, me))

    def l_copy(b, start, stop):
        piece = (pl.ds(start, stop - start), pl.ds(0, BLOCK * (b + 1)))
        return pltpu.make_async_remote_copy(
            src_ref=linv.at[piece], dst_ref=linvp.at[piece], send_sem=lsend.at[b], recv_sem=lrecv.at[b],
            device_id=(sector + 1, me), device_id_type=MESH)

    def carry(c):
        cols = columns[c]
        loads[1 + c].wait()
        mask(rv, 1, c)
        cs[:, cols] = nn(xv[...], rv[:, cols]).astype(BF16)

    full[...] = jnp.zeros((N, LANES), F32)
    loads[0].wait()
    for c in range(EARLY):
        carry(c)
    pl.semaphore_wait(barrier, count - 1 + above + below)

    @pl.when(has_last)
    def _():
        for c in range(NCH):
            x_copy(c).start()

    @pl.when(has_next)
    def _():
        for c in range(EARLY):
            c_copy(c).start()

    for c in range(EARLY, NCH):
        carry(c)

        @pl.when(has_next)
        def _():
            c_copy(c).start()

    for c, cols in enumerate(columns):
        loads[1 + NCH + c].wait()
        mask(dv, 0, c)
        acc[:, cols] = nn(xv[...], dv[:, cols])

    for c, cols in enumerate(columns):
        @pl.when(has_next)
        def _():
            x_copy(c).wait_recv()
            for out in columns:
                acc[:, out] += nt(xn[:, cols], rv[out, cols])

    gram = None
    for c, cols in enumerate(columns):
        @pl.when(has_last)
        def _():
            c_copy(c).wait_recv()
            acc[:, cols] += cr[:, cols].astype(F32)

        y = acc[:, cols].astype(BF16)
        yv[:, cols] = y

        @pl.when(z_sends)
        def _():
            z_copy(c).start()

        g = nt(y, y)
        gram = g if gram is None else gram + g

    scale = 1.0 / (count * ROWS)
    full[0:C, 0:C] = gram
    pack_symmetric(full, part)
    size_h, size_c = SYM // count, CROSS // count

    def chunk(index, size):
        return pl.ds(pl.multiple_of(index * size, 8), size)

    def gram_copy(k):
        peer = lax.rem(me + k, count)
        return pltpu.make_async_remote_copy(
            src_ref=part.at[chunk(peer, size_h)], dst_ref=recv.at[k], send_sem=a1, recv_sem=a2,
            device_id=(sector, peer), device_id_type=MESH)

    def gram_all(k):
        peer = lax.rem(me + k, count)
        mine = total.at[chunk(me, size_h)]
        return pltpu.make_async_remote_copy(
            src_ref=mine, dst_ref=mine, send_sem=a3, recv_sem=a4, device_id=(sector, peer), device_id_type=MESH)

    others = pl.ds(1, count - 1)
    each(1, count, lambda k: gram_copy(k).start())
    recv[0] = part[chunk(me, size_h), :]
    full[0:C, 0:C] = nt(xv[...], yv[...])
    pack_symmetric(full, part_h)
    take(recv.at[others], a2)
    total[chunk(me, size_h), :] = jnp.sum(recv[...], axis=0) * scale
    each(1, count, lambda k: gram_all(k).start())

    def h_copy(k):
        peer = lax.rem(me + k, count)
        return pltpu.make_async_remote_copy(
            src_ref=part_h.at[chunk(peer, size_h)], dst_ref=recv_h.at[k], send_sem=h1, recv_sem=h2,
            device_id=(sector, peer), device_id_type=MESH)

    def cross_copy(k):
        peer = lax.rem(me + k, count)
        return pltpu.make_async_remote_copy(
            src_ref=part_c.at[chunk(peer, size_c)], dst_ref=recv_c.at[k], send_sem=c1, recv_sem=c2,
            device_id=(sector + core, peer), device_id_type=MESH)

    def all_copy(k):
        peer = lax.rem(me + k, count)
        return pltpu.make_async_remote_copy(
            src_ref=total2.at[me], dst_ref=total2.at[me], send_sem=b1, recv_sem=b2,
            device_id=(sector, peer), device_id_type=MESH)

    each(1, count, lambda k: h_copy(k).start())
    recv_h[0] = part_h[chunk(me, size_h), :]
    full[...] = jnp.zeros((N, LANES), F32)
    for c, cols in enumerate(columns):
        @pl.when(z_arrives)
        def _():
            z_copy(c).wait_recv()

        @pl.when(z_arrives & (core == 0))
        def _():
            full[0:C, 0:C] += nt(yp[:, cols], yv[:, cols])

        @pl.when(z_arrives & (core == 1))
        def _():
            full[0:C, 0:C] += nt(yv[:, cols], yp[:, cols])

    part_c[0:N, :] = full[:, 0:128]
    part_c[N:2 * N, :] = full[:, 128:256]
    part_c[2 * N:2 * N + 152, :] = full[0:152, 256:384] + pltpu.roll(full[152:304, 256:384], 64, 1)
    part_c[2 * N + 152:CROSS, :] = jnp.zeros((8, BLOCK), F32)

    @pl.when(z_arrives)
    def _():
        each(1 - core, count, lambda k: cross_copy(k).start())

    @pl.when(core == 0)
    def _():
        recv_c[0] = part_c[chunk(me, size_c), :]

    def take_cross(sem):
        @pl.when(core == 0)
        def _():
            take(recv_c.at[others], sem)

        @pl.when(core == 1)
        def _():
            take(recv_c, sem)

    def gather_both():
        take(recv_h.at[others], h2)
        total2[me, 0:size_h, :] = jnp.sum(recv_h[...], axis=0) * scale

        @pl.when(has_down)
        def _():
            take_cross(c2)
            total2[me, size_h:size_h + size_c, :] = jnp.sum(recv_c[...], axis=0) * scale

        @pl.when(sector == 0)
        def _():
            total2[me, size_h:size_h + size_c, :] = jnp.zeros((size_c, BLOCK), F32)

        each(1, count, lambda k: all_copy(k).start())

    take(recv.at[others], a4)
    b00, b01, b11, b02, b12, b22 = unpack_upper(total)
    w[...] = jnp.zeros((3, N, BLOCK), F32)
    w[0, 0:128, :] = b00
    w[1, 0:128, :] = b01
    w[2, 0:128, :] = b02
    w[1, 128:256, :] = b11
    w[2, 128:256, :] = b12
    extra = (iota((48, 128), 0) == iota((48, 128), 1)) & (iota((48, 128), 0) >= 44)
    w[2, 256:304, :] = jnp.where(extra, 1.0, b22)

    for b, start, stop in SPANS:
        factor_block(w, b, (stop - start) // 8)
        if b < 2:
            later_rows(w, b)
        for t in range(3):
            shape = (stop - start, BLOCK)
            keep = iota(shape, 1) + BLOCK * t <= iota(shape, 0) + start
            linv[start:stop, BLOCK * t:BLOCK * (t + 1)] = jnp.where(keep, w[t, start:stop, :], 0.0)

        @pl.when(has_up)
        def _():
            l_copy(b, start, stop).start()

        if b == 0:
            gather_both()

    outs = []
    high, low = split(linv[...])
    for c, cols in enumerate(columns):
        block = yv[:, cols]
        qv[:, cols] = (nn(high[0:C, 0:C], block) + nn(low[0:C, 0:C], block)).astype(BF16)
        piece = pl.ds(c * CHUNK, CHUNK)
        outs.append(pltpu.make_async_copy(qv.at[:, piece], q_out.at[:, piece], outsem.at[c]))
        outs[-1].start()

    take(total2.at[others], b2)
    outs.append(pltpu.make_async_copy(total2, sums_out, outsem.at[NCH]))
    outs[-1].start()
    cross = total2[:, size_h:, :].reshape(CROSS, BLOCK)
    full[:, 0:128] = cross[0:N]
    full[:, 128:256] = cross[N:2 * N]
    last = cross[2 * N:2 * N + 152]
    left = iota((152, BLOCK), 1) < 64
    full[0:152, 256:384] = jnp.where(left, last, 0.0)
    full[152:304, 256:384] = jnp.where(left, pltpu.roll(last, 64, 1), 0.0)
    right[:, 0:N] = nt(full[...], linv[...], HI)
    right[:, N:] = jnp.zeros((N, LANES - N), F32)
    outs.append(pltpu.make_async_copy(right, right_out, outsem.at[NCH + 1]))
    outs[-1].start()

    @pl.when(has_down)
    def _():
        for span in SPANS:
            l_copy(*span).wait_recv()

    outs.append(pltpu.make_async_copy(linvp, linvp_out, outsem.at[NCH + 2]))
    outs[-1].start()
    for copy in outs:
        copy.wait()

    for c in range(NCH):
        @pl.when(has_last)
        def _():
            x_copy(c).wait_send()

        @pl.when(has_next)
        def _():
            c_copy(c).wait_send()

        @pl.when(z_sends)
        def _():
            z_copy(c).wait_send()

    @pl.when(has_up)
    def _():
        for span in SPANS:
            l_copy(*span).wait_send()

    take(recv.at[others], a1)
    take(recv.at[others], a3)
    take(recv_h.at[others], h1)
    take(total2.at[others], b1)

    @pl.when(z_arrives)
    def _():
        take_cross(c1)


def finish_kernel(q_in, sums_in, right_in, linvp_in, q_out, h_out, c_out, sums, right, linvp, full, q, sem):
    pairs = ((q_in, q), (sums_in, sums), (right_in, right), (linvp_in, linvp))
    copies = [pltpu.make_async_copy(*pair, sem.at[i]) for i, pair in enumerate(pairs)]
    for copy in copies:
        copy.start()
    copies[0].wait()
    q_copy = pltpu.make_async_copy(q, q_out, sem.at[4])
    q_copy.start()
    for copy in copies[1:]:
        copy.wait()
    size = SYM // sums.shape[0]
    c_out[:, 0, :] = nn(linvp[:, 0:N], right[:, 0:N], HI)[0:C, 0:C]
    b00, b01, b11, b02, b12, b22 = unpack_upper(sums[:, 0:size, :].reshape(SYM, BLOCK))
    full[0:128, 0:128] = b00
    full[0:128, 128:256] = b01
    full[0:128, 256:384] = b02
    full[128:256, 0:128] = b01.T
    full[128:256, 128:256] = b11
    full[128:256, 256:384] = b12
    full[256:304, 0:128] = b02.T[0:48]
    full[256:304, 128:256] = b12.T[0:48]
    full[256:304, 256:384] = b22
    h_out[:, 0, :] = full[0:C, 0:C]
    q_copy.wait()


def finish(q, sums, right, linvp):
    vmem = pl.BlockSpec(memory_space=pltpu.VMEM)
    anywhere = pl.BlockSpec(memory_space=pl.ANY)
    square = jax.ShapeDtypeStruct((C, 1, C), F32)
    return pl.pallas_call(
        finish_kernel, out_shape=(jax.ShapeDtypeStruct((C, ROWS), BF16), square, square),
        in_specs=[anywhere] * 4, out_specs=(anywhere, vmem, vmem),
        scratch_shapes=[pltpu.VMEM(sums.shape, F32)] + [pltpu.VMEM((N, LANES), F32)] * 3
        + [pltpu.VMEM((C, ROWS), BF16), pltpu.SemaphoreType.DMA((5,))],
        compiler_params=pltpu.CompilerParams(vmem_limit_bytes=57 << 20), name="finish",
    )(q, sums, right, linvp)


def shards(x_block, h_diag, h_right, pattern):
    count, sectors = lax.axis_size("rows"), lax.axis_size("sector")
    dma = pltpu.SemaphoreType.DMA
    vmem = pl.BlockSpec(memory_space=pltpu.VMEM)
    rows_b, square, size = (C, ROWS), (ROWS, ROWS), SYM + CROSS
    q, sums, right, linvp = pl.pallas_call(
        lambda *refs: kernel(count, sectors, *refs),
        out_shape=(jax.ShapeDtypeStruct((C, ROWS), BF16), jax.ShapeDtypeStruct((count, size // count, BLOCK), F32),
                   jax.ShapeDtypeStruct((N, LANES), F32), jax.ShapeDtypeStruct((N, LANES), F32)),
        in_specs=[pl.BlockSpec(memory_space=pltpu.SMEM)] + [pl.BlockSpec(memory_space=pl.ANY)] * 3,
        out_specs=(pl.BlockSpec(memory_space=pl.ANY),) * 4,
        scratch_shapes=[
            pltpu.VMEM(rows_b, BF16), pltpu.VMEM(rows_b, BF16), pltpu.VMEM(square, BF16), pltpu.VMEM(square, BF16),
            pltpu.VMEM(rows_b, F32), pltpu.VMEM(rows_b, BF16), pltpu.VMEM(rows_b, BF16), pltpu.VMEM(rows_b, BF16),
            pltpu.VMEM(rows_b, BF16), pltpu.VMEM((N, LANES), F32),
            pltpu.VMEM((SYM, BLOCK), F32), pltpu.VMEM((count, SYM // count, BLOCK), F32), pltpu.VMEM((SYM, BLOCK), F32),
            pltpu.VMEM((SYM, BLOCK), F32), pltpu.VMEM((count, SYM // count, BLOCK), F32),
            pltpu.VMEM((CROSS, BLOCK), F32), pltpu.VMEM((count, CROSS // count, BLOCK), F32),
            pltpu.VMEM((count, size // count, BLOCK), F32),
            pltpu.VMEM((3, N, BLOCK), F32), pltpu.VMEM((N, LANES), F32), pltpu.VMEM((N, LANES), F32),
            pltpu.VMEM(rows_b, BF16), pltpu.VMEM((N, LANES), F32),
            dma((1 + 2 * NCH,)), dma((NCH,)), dma((NCH,)), dma((NCH,)), dma((NCH,)), dma((NCH,)), dma((NCH,)),
            dma((3,)), dma((3,)), dma((NCH + 3,)),
        ] + [dma] * 10,
        compiler_params=pltpu.CompilerParams(collective_id=0, has_side_effects=True, vmem_limit_bytes=57 << 20),
        name="step",
    )(jnp.swapaxes(pattern[0], 0, 1), x_block[0].T, h_diag[0], h_right[0])
    q, h, corr = finish(q, sums, right, linvp)
    return q.T[None], jnp.swapaxes(h, 0, 1), jnp.swapaxes(corr, 0, 1)


def solution(mesh):
    in_specs = (
        P("sector", "rows", None),
        P("sector", "rows", None),
        P("sector", "rows", None),
        P("sector", None, "rows", None),
    )
    out_specs = (P("sector", "rows", None), P("sector", None, None), P("sector", None, None))
    return jax.shard_map(shards, mesh=mesh, in_specs=in_specs, out_specs=out_specs, check_vma=False)
```

```python
import jax
import jax.numpy as jnp
from jax import lax
from jax.experimental import pallas as pl
from jax.experimental.pallas import tpu as pltpu
from jax.sharding import PartitionSpec as P

HI = lax.Precision.HIGHEST
MESH = pl.DeviceIdType.MESH
F32 = jnp.float32
BF16 = jnp.bfloat16
N = 304
LANES = 384
C = 300
ROWS = 1280
CHUNK = 256
NCH = ROWS // CHUNK
BLOCK = 128


def nt(a, b, precision=None):
    return lax.dot_general(a, b, (((1,), (1,)), ((), ())), precision=precision, preferred_element_type=F32)


def tn(a, b, precision=None):
    return lax.dot_general(a, b, (((0,), (0,)), ((), ())), precision=precision, preferred_element_type=F32)


def nn(a, b, precision=None):
    return lax.dot_general(a, b, (((1,), (0,)), ((), ())), precision=precision, preferred_element_type=F32)


def panel_block(tiles, base_lane, count):
    lane = lax.broadcasted_iota(jnp.int32, (8, 128), 1)
    sub = lax.broadcasted_iota(jnp.int32, (8, 128), 0)
    ntile = len(tiles[0])
    for k in range(count):
        lo = 8 * k
        inside = (lane >= lo) & (lane < lo + 8)
        P = tiles[k]
        rows = [[jnp.broadcast_to(P[t][q:q + 1, :], (8, 128)) for t in range(ntile)] for q in range(8)]
        s = [[jnp.broadcast_to(rows[q][0][:, lo + p:lo + p + 1], (8, 128)) if p >= q else None for p in range(8)] for q in range(8)]
        for q in range(8):
            rows[q][0] = jnp.where(inside, jnp.where(lane == lo + q, 1.0, 0.0), rows[q][0])
        u = [[None] * 8 for _ in range(8)]
        rs = [None] * 8
        for p in range(8):
            rs[p] = lax.rsqrt(s[p][p])
            for r in range(p + 1, 8):
                u[p][r] = s[p][r] * rs[p]
            for q in range(p + 1, 8):
                for r in range(q, 8):
                    s[q][r] = s[q][r] - u[p][q] * u[p][r]
            rows[p] = [x * rs[p] for x in rows[p]]
            for q in range(p + 1, 8):
                rows[q] = [x - u[p][q] * y for x, y in zip(rows[q], rows[p])]
        fin = []
        for t in range(ntile):
            acc = rows[0][t]
            for q in range(1, 8):
                acc = jnp.where(sub == q, rows[q][t], acc)
            fin.append(acc)
        tiles[k] = fin
        for g in range(k + 1, count):
            cols = []
            for p in range(8):
                c = jnp.broadcast_to(tiles[g][0][:, lo + p:lo + p + 1], (8, 128))
                for q in range(p):
                    c = c - cols[q] * u[q][p]
                cols.append(c * rs[p])
            new = list(tiles[g])
            new[0] = jnp.where(inside, 0.0, new[0])
            for t in range(ntile):
                acc = new[t]
                for p in range(8):
                    acc = acc - cols[p] * rows[p][t]
                new[t] = acc
            tiles[g] = new
    return tiles


def iota(shape, dim):
    return lax.broadcasted_iota(jnp.int32, shape, dim)


def pack_symmetric(full, out):
    corner = pltpu.roll(full[256:304, 256:384], 0, 1)
    out[0:80, :] = full[0:80, 0:128]
    low = full[80:128, 0:128]
    out[80:128, :] = jnp.where(iota((48, 128), 1) < 48, corner, low)
    out[128:256, :] = full[0:128, 128:256]
    out[256:384, :] = full[128:256, 128:256]
    out[384:512, :] = full[0:128, 256:384] + pltpu.roll(full[128:256, 256:384], 64, 1)


def unpack_upper(packed):
    top = packed[0:128, :]
    upper = iota((128, 128), 1) >= iota((128, 128), 0)
    b00 = jnp.where(upper, top, top.T)
    b22 = jnp.where(iota((48, 128), 1) < 44, top[80:128, :], 0.0)
    both = packed[384:512, :]
    left = iota((128, 128), 1) < 64
    b02 = jnp.where(left, both, 0.0)
    b12 = jnp.where(left, pltpu.roll(both, 64, 1), 0.0)
    return b00, packed[128:256, :], packed[256:384, :], b02, b12, b22


def split(value):
    high = value.astype(BF16)
    return high, (value - high.astype(F32)).astype(BF16)


def factor_block(w, b, count):
    r0 = BLOCK * b
    order = [b] + [t for t in range(3) if t != b]
    tiles = [[w[t, r0 + 8 * g:r0 + 8 * g + 8, :] for t in order] for g in range(count)]
    tiles = panel_block(tiles, r0, count)
    for g in range(count):
        for i, t in enumerate(order):
            w[t, r0 + 8 * g:r0 + 8 * g + 8, :] = tiles[g][i]


def later_rows(w, b):
    r0, r1 = BLOCK * b, BLOCK * (b + 1)
    left = jnp.concatenate([w[t, r0:r1, :] for t in range(b + 1, 3)], axis=1)
    for t in range(3):
        right = w[t, r0:r1, :]
        if t == b:
            right = jnp.where(iota((BLOCK, BLOCK), 1) <= iota((BLOCK, BLOCK), 0), right, 0.0)
        update = tn(left, right, HI)[:N - r1]
        w[t, r1:N, :] = -update if t == b else w[t, r1:N, :] - update


def take(view, sem):
    pltpu.make_async_copy(view, view, sem).wait()


def each(lower, upper, action):
    def body(k, carry):
        action(k)
        return carry

    lax.fori_loop(lower, upper, body, 0)


SYM = 512
CROSS = 768
EARLY = 3
SIDE = 4
OFFSETS = sorted(
    [(dx, dy, dc) for dx in range(SIDE) for dy in range(SIDE) for dc in range(2) if (dx, dy, dc) != (0, 0, 0)],
    key=lambda d: -(min(d[0], SIDE - d[0]) + min(d[1], SIDE - d[1])))
SPANS = ((0, 0, 128), (1, 128, 256), (2, 256, 304))


def kernel(count, sectors, pattern, x_hbm, d_hbm, r_hbm, q_out, sums_out, right_out, linvp_out,
           xv, xn, dv, rv, acc, cs, cr, yv, yp, full, part, recv, total, part_h, recv_h, part_c, recv_c, total2, w, linv, linvp, qv, right,
           load, xsend, xrecv, csend, crecv, zsend, zrecv, lsend, lrecv, outsem, a1, a2, a3, a4, h1, h2, c1, c2, b1, b2):
    me = lax.axis_index("rows")
    sector = lax.axis_index("sector")
    has_next, has_last = me < count - 1, me > 0
    has_up, has_down = sector < sectors - 1, sector > 0
    core = lax.rem(me, 2)
    z_sends = ((core == 0) & has_up) | ((core == 1) & has_down)
    z_arrives = ((core == 0) & has_down) | ((core == 1) & has_up)
    columns = [slice(c * CHUNK, (c + 1) * CHUNK) for c in range(NCH)]

    loads = [pltpu.make_async_copy(x_hbm, xv, load.at[0])]
    for i, (source, target) in enumerate(((r_hbm, rv), (d_hbm, dv))):
        for c in range(NCH):
            cols = pl.ds(c * CHUNK, CHUNK)
            loads.append(pltpu.make_async_copy(source.at[:, cols], target.at[:, cols], load.at[1 + i * NCH + c]))
    for l in loads:
        l.start()
    linvp[...] = jnp.zeros((N, LANES), F32)

    barrier = pltpu.get_barrier_semaphore()

    def signal(k, carry):
        pl.semaphore_signal(barrier, inc=1, device_id=(sector, lax.rem(me + k, count)), device_id_type=MESH)
        return carry

    lax.fori_loop(1, count, signal, 0)

    @pl.when(has_down)
    def _():
        def signal_below(k, carry):
            pl.semaphore_signal(barrier, inc=1, device_id=(sector - 1, 2 * k + 1), device_id_type=MESH)
            return carry

        lax.fori_loop(0, count // 2, signal_below, 0)

    @pl.when(has_down & (core == 0))
    def _():
        pl.semaphore_signal(barrier, inc=1, device_id=(sector - 1, me), device_id_type=MESH)

    @pl.when(has_up & (core == 1))
    def _():
        pl.semaphore_signal(barrier, inc=1, device_id=(sector + 1, me), device_id_type=MESH)

    above = jnp.where(has_up, jnp.where(core == 1, count, 1), 0)
    below = jnp.where(has_down & (core == 1), 1, 0)
    def mask(tile, which, c):
        for i in range(ROWS // BLOCK):
            for j in range(CHUNK // BLOCK):
                row = slice(i * BLOCK, (i + 1) * BLOCK)
                col = slice(c * CHUNK + j * BLOCK, c * CHUNK + (j + 1) * BLOCK)
                keep = pattern[i, which, c * (CHUNK // BLOCK) + j]
                scale = jnp.full((BLOCK, BLOCK), keep.astype(F32)).astype(BF16)
                tile[row, col] = tile[row, col] * scale

    def remote(source, target, send, arrive, c, device):
        cols = pl.ds(c * CHUNK, CHUNK)
        return pltpu.make_async_remote_copy(
            src_ref=source.at[:, cols], dst_ref=target.at[:, cols], send_sem=send.at[c], recv_sem=arrive.at[c],
            device_id=device, device_id_type=MESH)

    def x_copy(c):
        return remote(x_hbm, xn, xsend, xrecv, c, (sector, me - 1))

    def c_copy(c):
        return remote(cs, cr, csend, crecv, c, (sector, me + 1))

    def z_copy(c):
        return remote(yv, yp, zsend, zrecv, c, (sector + 1 - 2 * core, me))

    def l_copy(b, start, stop):
        piece = (pl.ds(start, stop - start), pl.ds(0, BLOCK * (b + 1)))
        return pltpu.make_async_remote_copy(
            src_ref=linv.at[piece], dst_ref=linvp.at[piece], send_sem=lsend.at[b], recv_sem=lrecv.at[b],
            device_id=(sector + 1, me), device_id_type=MESH)

    def carry(c):
        cols = columns[c]
        loads[1 + c].wait()
        mask(rv, 1, c)
        cs[:, cols] = nn(xv[...], rv[:, cols]).astype(BF16)

    full[...] = jnp.zeros((N, LANES), F32)
    loads[0].wait()
    for c in range(EARLY):
        carry(c)
    pl.semaphore_wait(barrier, count - 1 + above + below)

    @pl.when(has_last)
    def _():
        for c in range(NCH):
            x_copy(c).start()

    @pl.when(has_next)
    def _():
        for c in range(EARLY):
            c_copy(c).start()

    for c in range(EARLY, NCH):
        carry(c)

        @pl.when(has_next)
        def _():
            c_copy(c).start()

    for c, cols in enumerate(columns):
        loads[1 + NCH + c].wait()
        mask(dv, 0, c)
        acc[:, cols] = nn(xv[...], dv[:, cols])

    for c, cols in enumerate(columns):
        @pl.when(has_next)
        def _():
            x_copy(c).wait_recv()
            for out in columns:
                acc[:, out] += nt(xn[:, cols], rv[out, cols])

    gram = None
    for c, cols in enumerate(columns):
        @pl.when(has_last)
        def _():
            c_copy(c).wait_recv()
            acc[:, cols] += cr[:, cols].astype(F32)

        y = acc[:, cols].astype(BF16)
        yv[:, cols] = y

        @pl.when(z_sends)
        def _():
            z_copy(c).start()

        g = nt(y, y)
        gram = g if gram is None else gram + g

    scale = 1.0 / (count * ROWS)
    full[0:C, 0:C] = gram
    pack_symmetric(full, part)
    size_h, size_c = SYM // count, CROSS // count

    def chunk(index, size):
        return pl.ds(pl.multiple_of(index * size, 8), size)

    along_x = [lax.rem(me // (2 * SIDE) + d, SIDE) * (2 * SIDE) for d in range(SIDE)]
    along_y = [lax.rem(me // 2 + d, SIDE) * 2 for d in range(SIDE)]
    along_c = [core, 1 - core]

    def peer_of(k):
        dx, dy, dc = OFFSETS[k - 1]
        return along_x[dx] + along_y[dy] + along_c[dc]

    def gram_copy(k):
        peer = peer_of(k)
        return pltpu.make_async_remote_copy(
            src_ref=part.at[chunk(peer, size_h)], dst_ref=recv.at[k], send_sem=a1, recv_sem=a2,
            device_id=(sector, peer), device_id_type=MESH)

    def gram_all(k):
        peer = peer_of(k)
        mine = total.at[chunk(me, size_h)]
        return pltpu.make_async_remote_copy(
            src_ref=mine, dst_ref=mine, send_sem=a3, recv_sem=a4, device_id=(sector, peer), device_id_type=MESH)

    others = pl.ds(1, count - 1)
    for k in range(1, count):
        gram_copy(k).start()
    recv[0] = part[chunk(me, size_h), :]
    full[0:C, 0:C] = nt(xv[...], yv[...])
    pack_symmetric(full, part_h)
    take(recv.at[others], a2)
    total[chunk(me, size_h), :] = jnp.sum(recv[...], axis=0) * scale
    for k in range(1, count):
        gram_all(k).start()

    def h_copy(k):
        peer = lax.rem(me + k, count)
        return pltpu.make_async_remote_copy(
            src_ref=part_h.at[chunk(peer, size_h)], dst_ref=recv_h.at[k], send_sem=h1, recv_sem=h2,
            device_id=(sector, peer), device_id_type=MESH)

    def cross_copy(k):
        peer = lax.rem(me + k, count)
        return pltpu.make_async_remote_copy(
            src_ref=part_c.at[chunk(peer, size_c)], dst_ref=recv_c.at[k], send_sem=c1, recv_sem=c2,
            device_id=(sector + core, peer), device_id_type=MESH)

    def all_copy(k):
        peer = peer_of(k)
        return pltpu.make_async_remote_copy(
            src_ref=total2.at[me], dst_ref=total2.at[me], send_sem=b1, recv_sem=b2,
            device_id=(sector, peer), device_id_type=MESH)

    each(1, count, lambda k: h_copy(k).start())
    recv_h[0] = part_h[chunk(me, size_h), :]
    full[...] = jnp.zeros((N, LANES), F32)
    for c, cols in enumerate(columns):
        @pl.when(z_arrives)
        def _():
            z_copy(c).wait_recv()

        @pl.when(z_arrives & (core == 0))
        def _():
            full[0:C, 0:C] += nt(yp[:, cols], yv[:, cols])

        @pl.when(z_arrives & (core == 1))
        def _():
            full[0:C, 0:C] += nt(yv[:, cols], yp[:, cols])

    part_c[0:N, :] = full[:, 0:128]
    part_c[N:2 * N, :] = full[:, 128:256]
    part_c[2 * N:2 * N + 152, :] = full[0:152, 256:384] + pltpu.roll(full[152:304, 256:384], 64, 1)
    part_c[2 * N + 152:CROSS, :] = jnp.zeros((8, BLOCK), F32)

    @pl.when(z_arrives)
    def _():
        each(1 - core, count, lambda k: cross_copy(k).start())

    @pl.when(core == 0)
    def _():
        recv_c[0] = part_c[chunk(me, size_c), :]

    def take_cross(sem):
        @pl.when(core == 0)
        def _():
            take(recv_c.at[others], sem)

        @pl.when(core == 1)
        def _():
            take(recv_c, sem)

    def gather_both():
        take(recv_h.at[others], h2)
        total2[me, 0:size_h, :] = jnp.sum(recv_h[...], axis=0) * scale

        @pl.when(has_down)
        def _():
            take_cross(c2)
            total2[me, size_h:size_h + size_c, :] = jnp.sum(recv_c[...], axis=0) * scale

        @pl.when(sector == 0)
        def _():
            total2[me, size_h:size_h + size_c, :] = jnp.zeros((size_c, BLOCK), F32)

        for k in range(1, count):
            all_copy(k).start()

    take(recv.at[others], a4)
    b00, b01, b11, b02, b12, b22 = unpack_upper(total)
    w[...] = jnp.zeros((3, N, BLOCK), F32)
    w[0, 0:128, :] = b00
    w[1, 0:128, :] = b01
    w[2, 0:128, :] = b02
    w[1, 128:256, :] = b11
    w[2, 128:256, :] = b12
    extra = (iota((48, 128), 0) == iota((48, 128), 1)) & (iota((48, 128), 0) >= 44)
    w[2, 256:304, :] = jnp.where(extra, 1.0, b22)

    for b, start, stop in SPANS:
        factor_block(w, b, (stop - start) // 8)
        if b < 2:
            later_rows(w, b)
        for t in range(3):
            shape = (stop - start, BLOCK)
            keep = iota(shape, 1) + BLOCK * t <= iota(shape, 0) + start
            linv[start:stop, BLOCK * t:BLOCK * (t + 1)] = jnp.where(keep, w[t, start:stop, :], 0.0)

        @pl.when(has_up)
        def _():
            l_copy(b, start, stop).start()

        if b == 0:
            gather_both()

    outs = []
    high, low = split(linv[...])
    for c, cols in enumerate(columns):
        block = yv[:, cols]
        qv[:, cols] = (nn(high[0:C, 0:C], block) + nn(low[0:C, 0:C], block)).astype(BF16)
        piece = pl.ds(c * CHUNK, CHUNK)
        outs.append(pltpu.make_async_copy(qv.at[:, piece], q_out.at[:, piece], outsem.at[c]))
        outs[-1].start()

    take(total2.at[others], b2)
    outs.append(pltpu.make_async_copy(total2, sums_out, outsem.at[NCH]))
    outs[-1].start()
    cross = total2[:, size_h:, :].reshape(CROSS, BLOCK)
    full[:, 0:128] = cross[0:N]
    full[:, 128:256] = cross[N:2 * N]
    last = cross[2 * N:2 * N + 152]
    left = iota((152, BLOCK), 1) < 64
    full[0:152, 256:384] = jnp.where(left, last, 0.0)
    full[152:304, 256:384] = jnp.where(left, pltpu.roll(last, 64, 1), 0.0)
    right[:, 0:N] = nt(full[...], linv[...], HI)
    right[:, N:] = jnp.zeros((N, LANES - N), F32)
    outs.append(pltpu.make_async_copy(right, right_out, outsem.at[NCH + 1]))
    outs[-1].start()

    @pl.when(has_down)
    def _():
        for span in SPANS:
            l_copy(*span).wait_recv()

    outs.append(pltpu.make_async_copy(linvp, linvp_out, outsem.at[NCH + 2]))
    outs[-1].start()
    for copy in outs:
        copy.wait()

    for c in range(NCH):
        @pl.when(has_last)
        def _():
            x_copy(c).wait_send()

        @pl.when(has_next)
        def _():
            c_copy(c).wait_send()

        @pl.when(z_sends)
        def _():
            z_copy(c).wait_send()

    @pl.when(has_up)
    def _():
        for span in SPANS:
            l_copy(*span).wait_send()

    take(recv.at[others], a1)
    take(recv.at[others], a3)
    take(recv_h.at[others], h1)
    take(total2.at[others], b1)

    @pl.when(z_arrives)
    def _():
        take_cross(c1)


def finish_kernel(q_in, sums_in, right_in, linvp_in, q_out, h_out, c_out, sums, right, linvp, full, h, corr, q, sem, q_sem):
    pairs = ((sums_in, sums), (right_in, right), (linvp_in, linvp))
    copies = [pltpu.make_async_copy(*pair, sem.at[i]) for i, pair in enumerate(pairs)]

    def q_copy(source, target, c, way):
        piece = pl.ds(c * CHUNK, CHUNK)
        return pltpu.make_async_copy(source.at[:, piece], target.at[:, piece], q_sem.at[way, c])

    copies[0].start()
    for c in range(NCH):
        q_copy(q_in, q, c, 0).start()
    for copy in copies[1:]:
        copy.start()
    for c in range(NCH):
        q_copy(q_in, q, c, 0).wait()
        q_copy(q, q_out, c, 1).start()
    copies[0].wait()
    size = SYM // sums.shape[0]
    b00, b01, b11, b02, b12, b22 = unpack_upper(sums[:, 0:size, :].reshape(SYM, BLOCK))
    full[0:128, 0:128] = b00
    full[0:128, 128:256] = b01
    full[0:128, 256:384] = b02
    full[128:256, 0:128] = b01.T
    full[128:256, 128:256] = b11
    full[128:256, 256:384] = b12
    full[256:304, 0:128] = b02.T[0:48]
    full[256:304, 128:256] = b12.T[0:48]
    full[256:304, 256:384] = b22
    h[:, 0, :] = full[0:C, 0:C]
    h_copy = pltpu.make_async_copy(h, h_out, sem.at[3])
    h_copy.start()
    copies[1].wait()
    copies[2].wait()
    corr[:, 0, :] = nn(linvp[:, 0:N], right[:, 0:N], HI)[0:C, 0:C]
    c_copy = pltpu.make_async_copy(corr, c_out, sem.at[4])
    c_copy.start()
    for c in range(NCH):
        q_copy(q, q_out, c, 1).wait()
    h_copy.wait()
    c_copy.wait()


def finish(q, sums, right, linvp):
    anywhere = pl.BlockSpec(memory_space=pl.ANY)
    square = jax.ShapeDtypeStruct((C, 1, C), F32)
    return pl.pallas_call(
        finish_kernel, out_shape=(jax.ShapeDtypeStruct((C, ROWS), BF16), square, square),
        in_specs=[anywhere] * 4, out_specs=(anywhere,) * 3,
        scratch_shapes=[pltpu.VMEM(sums.shape, F32)] + [pltpu.VMEM((N, LANES), F32)] * 3
        + [pltpu.VMEM((C, 1, C), F32)] * 2
        + [pltpu.VMEM((C, ROWS), BF16), pltpu.SemaphoreType.DMA((5,)), pltpu.SemaphoreType.DMA((2, NCH))],
        compiler_params=pltpu.CompilerParams(vmem_limit_bytes=57 << 20), name="finish",
    )(q, sums, right, linvp)


def shards(x_block, h_diag, h_right, pattern):
    count, sectors = lax.axis_size("rows"), lax.axis_size("sector")
    dma = pltpu.SemaphoreType.DMA
    vmem = pl.BlockSpec(memory_space=pltpu.VMEM)
    rows_b, square, size = (C, ROWS), (ROWS, ROWS), SYM + CROSS
    q, sums, right, linvp = pl.pallas_call(
        lambda *refs: kernel(count, sectors, *refs),
        out_shape=(jax.ShapeDtypeStruct((C, ROWS), BF16), jax.ShapeDtypeStruct((count, size // count, BLOCK), F32),
                   jax.ShapeDtypeStruct((N, LANES), F32), jax.ShapeDtypeStruct((N, LANES), F32)),
        in_specs=[pl.BlockSpec(memory_space=pltpu.SMEM)] + [pl.BlockSpec(memory_space=pl.ANY)] * 3,
        out_specs=(pl.BlockSpec(memory_space=pl.ANY),) * 4,
        scratch_shapes=[
            pltpu.VMEM(rows_b, BF16), pltpu.VMEM(rows_b, BF16), pltpu.VMEM(square, BF16), pltpu.VMEM(square, BF16),
            pltpu.VMEM(rows_b, F32), pltpu.VMEM(rows_b, BF16), pltpu.VMEM(rows_b, BF16), pltpu.VMEM(rows_b, BF16),
            pltpu.VMEM(rows_b, BF16), pltpu.VMEM((N, LANES), F32),
            pltpu.VMEM((SYM, BLOCK), F32), pltpu.VMEM((count, SYM // count, BLOCK), F32), pltpu.VMEM((SYM, BLOCK), F32),
            pltpu.VMEM((SYM, BLOCK), F32), pltpu.VMEM((count, SYM // count, BLOCK), F32),
            pltpu.VMEM((CROSS, BLOCK), F32), pltpu.VMEM((count, CROSS // count, BLOCK), F32),
            pltpu.VMEM((count, size // count, BLOCK), F32),
            pltpu.VMEM((3, N, BLOCK), F32), pltpu.VMEM((N, LANES), F32), pltpu.VMEM((N, LANES), F32),
            pltpu.VMEM(rows_b, BF16), pltpu.VMEM((N, LANES), F32),
            dma((1 + 2 * NCH,)), dma((NCH,)), dma((NCH,)), dma((NCH,)), dma((NCH,)), dma((NCH,)), dma((NCH,)),
            dma((3,)), dma((3,)), dma((NCH + 3,)),
        ] + [dma] * 10,
        compiler_params=pltpu.CompilerParams(collective_id=0, has_side_effects=True, vmem_limit_bytes=57 << 20),
        name="step",
    )(jnp.swapaxes(pattern[0], 0, 1), x_block[0].T, h_diag[0], h_right[0])
    q, h, corr = finish(q, sums, right, linvp)
    return q.T[None], jnp.swapaxes(h, 0, 1), jnp.swapaxes(corr, 0, 1)


def solution(mesh):
    in_specs = (
        P("sector", "rows", None),
        P("sector", "rows", None),
        P("sector", "rows", None),
        P("sector", None, "rows", None),
    )
    out_specs = (P("sector", "rows", None), P("sector", None, None), P("sector", None, None))
    return jax.shard_map(shards, mesh=mesh, in_specs=in_specs, out_specs=out_specs, check_vma=False)
```

```python
import jax
import jax.numpy as jnp
from jax import lax
from jax.experimental import pallas as pl
from jax.experimental.pallas import tpu as pltpu
from jax.sharding import PartitionSpec as P

HI = lax.Precision.HIGHEST
MESH = pl.DeviceIdType.MESH
F32 = jnp.float32
BF16 = jnp.bfloat16
N = 304
LANES = 384
C = 300
ROWS = 1280
CHUNK = 256
NCH = ROWS // CHUNK
BLOCK = 128


def nt(a, b, precision=None):
    return lax.dot_general(a, b, (((1,), (1,)), ((), ())), precision=precision, preferred_element_type=F32)


def tn(a, b, precision=None):
    return lax.dot_general(a, b, (((0,), (0,)), ((), ())), precision=precision, preferred_element_type=F32)


def nn(a, b, precision=None):
    return lax.dot_general(a, b, (((1,), (0,)), ((), ())), precision=precision, preferred_element_type=F32)


def panel_block(tiles, base_lane, count):
    lane = lax.broadcasted_iota(jnp.int32, (8, 128), 1)
    sub = lax.broadcasted_iota(jnp.int32, (8, 128), 0)
    ntile = len(tiles[0])
    for k in range(count):
        lo = 8 * k
        inside = (lane >= lo) & (lane < lo + 8)
        P = tiles[k]
        rows = [[jnp.broadcast_to(P[t][q:q + 1, :], (8, 128)) for t in range(ntile)] for q in range(8)]
        s = [[jnp.broadcast_to(rows[q][0][:, lo + p:lo + p + 1], (8, 128)) if p >= q else None for p in range(8)] for q in range(8)]
        for q in range(8):
            rows[q][0] = jnp.where(inside, jnp.where(lane == lo + q, 1.0, 0.0), rows[q][0])
        u = [[None] * 8 for _ in range(8)]
        rs = [None] * 8
        for p in range(8):
            rs[p] = lax.rsqrt(s[p][p])
            for r in range(p + 1, 8):
                u[p][r] = s[p][r] * rs[p]
            for q in range(p + 1, 8):
                for r in range(q, 8):
                    s[q][r] = s[q][r] - u[p][q] * u[p][r]
            rows[p] = [x * rs[p] for x in rows[p]]
            for q in range(p + 1, 8):
                rows[q] = [x - u[p][q] * y for x, y in zip(rows[q], rows[p])]
        fin = []
        for t in range(ntile):
            acc = rows[0][t]
            for q in range(1, 8):
                acc = jnp.where(sub == q, rows[q][t], acc)
            fin.append(acc)
        tiles[k] = fin
        for g in range(k + 1, count):
            cols = []
            for p in range(8):
                c = jnp.broadcast_to(tiles[g][0][:, lo + p:lo + p + 1], (8, 128))
                for q in range(p):
                    c = c - cols[q] * u[q][p]
                cols.append(c * rs[p])
            new = list(tiles[g])
            new[0] = jnp.where(inside, 0.0, new[0])
            for t in range(ntile):
                acc = new[t]
                for p in range(8):
                    acc = acc - cols[p] * rows[p][t]
                new[t] = acc
            tiles[g] = new
    return tiles


def iota(shape, dim):
    return lax.broadcasted_iota(jnp.int32, shape, dim)


def pack_symmetric(full, out):
    corner = pltpu.roll(full[256:304, 256:384], 0, 1)
    out[0:80, :] = full[0:80, 0:128]
    low = full[80:128, 0:128]
    out[80:128, :] = jnp.where(iota((48, 128), 1) < 48, corner, low)
    out[128:256, :] = full[0:128, 128:256]
    out[256:384, :] = full[128:256, 128:256]
    out[384:512, :] = full[0:128, 256:384] + pltpu.roll(full[128:256, 256:384], 64, 1)


def unpack_upper(packed):
    top = packed[0:128, :]
    upper = iota((128, 128), 1) >= iota((128, 128), 0)
    b00 = jnp.where(upper, top, top.T)
    b22 = jnp.where(iota((48, 128), 1) < 44, top[80:128, :], 0.0)
    both = packed[384:512, :]
    left = iota((128, 128), 1) < 64
    b02 = jnp.where(left, both, 0.0)
    b12 = jnp.where(left, pltpu.roll(both, 64, 1), 0.0)
    return b00, packed[128:256, :], packed[256:384, :], b02, b12, b22


def split(value):
    high = value.astype(BF16)
    return high, (value - high.astype(F32)).astype(BF16)


def factor_block(w, b, count):
    r0 = BLOCK * b
    order = [b] + [t for t in range(3) if t != b]
    tiles = [[w[t, r0 + 8 * g:r0 + 8 * g + 8, :] for t in order] for g in range(count)]
    tiles = panel_block(tiles, r0, count)
    for g in range(count):
        for i, t in enumerate(order):
            w[t, r0 + 8 * g:r0 + 8 * g + 8, :] = tiles[g][i]


def later_rows(w, b):
    r0, r1 = BLOCK * b, BLOCK * (b + 1)
    left = jnp.concatenate([w[t, r0:r1, :] for t in range(b + 1, 3)], axis=1)
    for t in range(3):
        right = w[t, r0:r1, :]
        if t == b:
            right = jnp.where(iota((BLOCK, BLOCK), 1) <= iota((BLOCK, BLOCK), 0), right, 0.0)
        update = tn(left, right, HI)[:N - r1]
        w[t, r1:N, :] = -update if t == b else w[t, r1:N, :] - update


def take(view, sem):
    pltpu.make_async_copy(view, view, sem).wait()


def each(lower, upper, action):
    def body(k, carry):
        action(k)
        return carry

    lax.fori_loop(lower, upper, body, 0)


SYM = 512
CROSS = 768
EARLY = 3
SIDE = 4
OFFSETS = sorted(
    [(dx, dy, dc) for dx in range(SIDE) for dy in range(SIDE) for dc in range(2) if (dx, dy, dc) != (0, 0, 0)],
    key=lambda d: -(min(d[0], SIDE - d[0]) + min(d[1], SIDE - d[1])))
SPANS = ((0, 0, 128), (1, 128, 256), (2, 256, 304))


def kernel(count, sectors, pattern, x_hbm, d_hbm, r_hbm, q_out, sums_out, right_out, linvp_out,
           xv, xn, dv, rv, acc, cs, cr, yv, yp, full, part, recv, total, part_h, recv_h, part_c, recv_c, total2, w, linv, linvp, qv, right,
           load, xsend, xrecv, csend, crecv, zsend, zrecv, lsend, lrecv, outsem, a1, a2, a3, a4, h1, h2, c1, c2, b1, b2):
    me = lax.axis_index("rows")
    sector = lax.axis_index("sector")
    has_next, has_last = me < count - 1, me > 0
    has_up, has_down = sector < sectors - 1, sector > 0
    core = lax.rem(me, 2)
    z_sends = ((core == 0) & has_up) | ((core == 1) & has_down)
    z_arrives = ((core == 0) & has_down) | ((core == 1) & has_up)
    columns = [slice(c * CHUNK, (c + 1) * CHUNK) for c in range(NCH)]

    loads = [pltpu.make_async_copy(x_hbm, xv, load.at[0])]
    for i, (source, target) in enumerate(((r_hbm, rv), (d_hbm, dv))):
        for c in range(NCH):
            cols = pl.ds(c * CHUNK, CHUNK)
            loads.append(pltpu.make_async_copy(source.at[:, cols], target.at[:, cols], load.at[1 + i * NCH + c]))
    for l in loads:
        l.start()
    linvp[...] = jnp.zeros((N, LANES), F32)

    barrier = pltpu.get_barrier_semaphore()

    @pl.when(has_down)
    def _():
        for k in range(count // 2):
            pl.semaphore_signal(barrier, inc=1, device_id=(sector - 1, 2 * k + 1), device_id_type=MESH)

    @pl.when(has_down & (core == 0))
    def _():
        pl.semaphore_signal(barrier, inc=1, device_id=(sector - 1, me), device_id_type=MESH)

    @pl.when(has_up & (core == 1))
    def _():
        pl.semaphore_signal(barrier, inc=1, device_id=(sector + 1, me), device_id_type=MESH)

    along_x = [lax.rem(me // (2 * SIDE) + d, SIDE) * (2 * SIDE) for d in range(SIDE)]
    along_y = [lax.rem(me // 2 + d, SIDE) * 2 for d in range(SIDE)]
    along_c = [core, 1 - core]

    def peer_of(k):
        dx, dy, dc = OFFSETS[k - 1]
        return along_x[dx] + along_y[dy] + along_c[dc]

    for k in range(1, count):
        pl.semaphore_signal(barrier, inc=1, device_id=(sector, peer_of(k)), device_id_type=MESH)

    above = jnp.where(has_up, jnp.where(core == 1, count, 1), 0)
    below = jnp.where(has_down & (core == 1), 1, 0)
    def mask(tile, which, c):
        for i in range(ROWS // BLOCK):
            for j in range(CHUNK // BLOCK):
                row = slice(i * BLOCK, (i + 1) * BLOCK)
                col = slice(c * CHUNK + j * BLOCK, c * CHUNK + (j + 1) * BLOCK)
                keep = pattern[i, which, c * (CHUNK // BLOCK) + j]
                scale = jnp.full((BLOCK, BLOCK), keep.astype(F32)).astype(BF16)
                tile[row, col] = tile[row, col] * scale

    def remote(source, target, send, arrive, c, device):
        cols = pl.ds(c * CHUNK, CHUNK)
        return pltpu.make_async_remote_copy(
            src_ref=source.at[:, cols], dst_ref=target.at[:, cols], send_sem=send.at[c], recv_sem=arrive.at[c],
            device_id=device, device_id_type=MESH)

    def x_copy(c):
        return remote(x_hbm, xn, xsend, xrecv, c, (sector, me - 1))

    def c_copy(c):
        return remote(cs, cr, csend, crecv, c, (sector, me + 1))

    def z_copy(c):
        return remote(yv, yp, zsend, zrecv, c, (sector + 1 - 2 * core, me))

    def l_copy(b, start, stop):
        piece = (pl.ds(start, stop - start), pl.ds(0, BLOCK * (b + 1)))
        return pltpu.make_async_remote_copy(
            src_ref=linv.at[piece], dst_ref=linvp.at[piece], send_sem=lsend.at[b], recv_sem=lrecv.at[b],
            device_id=(sector + 1, me), device_id_type=MESH)

    def carry(c):
        cols = columns[c]
        loads[1 + c].wait()
        mask(rv, 1, c)
        cs[:, cols] = nn(xv[...], rv[:, cols]).astype(BF16)

    full[...] = jnp.zeros((N, LANES), F32)
    loads[0].wait()
    for c in range(EARLY):
        carry(c)
    pl.semaphore_wait(barrier, count - 1 + above + below)

    @pl.when(has_last)
    def _():
        for c in range(NCH):
            x_copy(c).start()

    @pl.when(has_next)
    def _():
        for c in range(EARLY):
            c_copy(c).start()

    for c in range(EARLY, NCH):
        carry(c)

        @pl.when(has_next)
        def _():
            c_copy(c).start()

    for c, cols in enumerate(columns):
        loads[1 + NCH + c].wait()
        mask(dv, 0, c)
        acc[:, cols] = nn(xv[...], dv[:, cols])

    for c, cols in enumerate(columns):
        @pl.when(has_next)
        def _():
            x_copy(c).wait_recv()
            for out in columns:
                acc[:, out] += nt(xn[:, cols], rv[out, cols])

    gram = None
    for c, cols in enumerate(columns):
        @pl.when(has_last)
        def _():
            c_copy(c).wait_recv()
            acc[:, cols] += cr[:, cols].astype(F32)

        y = acc[:, cols].astype(BF16)
        yv[:, cols] = y

        @pl.when(z_sends)
        def _():
            z_copy(c).start()

        g = nt(y, y)
        gram = g if gram is None else gram + g

    scale = 1.0 / (count * ROWS)
    full[0:C, 0:C] = gram
    pack_symmetric(full, part)
    size_h, size_c = SYM // count, CROSS // count

    def chunk(index, size):
        return pl.ds(pl.multiple_of(index * size, 8), size)

    def gram_copy(k):
        peer = peer_of(k)
        return pltpu.make_async_remote_copy(
            src_ref=part.at[chunk(peer, size_h)], dst_ref=recv.at[k], send_sem=a1, recv_sem=a2,
            device_id=(sector, peer), device_id_type=MESH)

    def gram_all(k):
        peer = peer_of(k)
        mine = total.at[chunk(me, size_h)]
        return pltpu.make_async_remote_copy(
            src_ref=mine, dst_ref=mine, send_sem=a3, recv_sem=a4, device_id=(sector, peer), device_id_type=MESH)

    others = pl.ds(1, count - 1)
    for k in range(1, count):
        gram_copy(k).start()
    recv[0] = part[chunk(me, size_h), :]
    full[0:C, 0:C] = nt(xv[...], yv[...])
    pack_symmetric(full, part_h)
    take(recv.at[others], a2)
    total[chunk(me, size_h), :] = jnp.sum(recv[...], axis=0) * scale
    for k in range(1, count):
        gram_all(k).start()

    def h_copy(k):
        peer = lax.rem(me + k, count)
        return pltpu.make_async_remote_copy(
            src_ref=part_h.at[chunk(peer, size_h)], dst_ref=recv_h.at[k], send_sem=h1, recv_sem=h2,
            device_id=(sector, peer), device_id_type=MESH)

    def cross_copy(k):
        peer = lax.rem(me + k, count)
        return pltpu.make_async_remote_copy(
            src_ref=part_c.at[chunk(peer, size_c)], dst_ref=recv_c.at[k], send_sem=c1, recv_sem=c2,
            device_id=(sector + core, peer), device_id_type=MESH)

    def all_copy(k):
        peer = peer_of(k)
        return pltpu.make_async_remote_copy(
            src_ref=total2.at[me], dst_ref=total2.at[me], send_sem=b1, recv_sem=b2,
            device_id=(sector, peer), device_id_type=MESH)

    each(1, count, lambda k: h_copy(k).start())
    recv_h[0] = part_h[chunk(me, size_h), :]
    full[...] = jnp.zeros((N, LANES), F32)
    for c, cols in enumerate(columns):
        @pl.when(z_arrives)
        def _():
            z_copy(c).wait_recv()

        @pl.when(z_arrives & (core == 0))
        def _():
            full[0:C, 0:C] += nt(yp[:, cols], yv[:, cols])

        @pl.when(z_arrives & (core == 1))
        def _():
            full[0:C, 0:C] += nt(yv[:, cols], yp[:, cols])

    part_c[0:N, :] = full[:, 0:128]
    part_c[N:2 * N, :] = full[:, 128:256]
    part_c[2 * N:2 * N + 152, :] = full[0:152, 256:384] + pltpu.roll(full[152:304, 256:384], 64, 1)
    part_c[2 * N + 152:CROSS, :] = jnp.zeros((8, BLOCK), F32)

    @pl.when(z_arrives)
    def _():
        each(1 - core, count, lambda k: cross_copy(k).start())

    @pl.when(core == 0)
    def _():
        recv_c[0] = part_c[chunk(me, size_c), :]

    def take_cross(sem):
        @pl.when(core == 0)
        def _():
            take(recv_c.at[others], sem)

        @pl.when(core == 1)
        def _():
            take(recv_c, sem)

    def gather_both():
        take(recv_h.at[others], h2)
        total2[me, 0:size_h, :] = jnp.sum(recv_h[...], axis=0) * scale

        @pl.when(has_down)
        def _():
            take_cross(c2)
            total2[me, size_h:size_h + size_c, :] = jnp.sum(recv_c[...], axis=0) * scale

        @pl.when(sector == 0)
        def _():
            total2[me, size_h:size_h + size_c, :] = jnp.zeros((size_c, BLOCK), F32)

        for k in range(1, count):
            all_copy(k).start()

    take(recv.at[others], a4)
    b00, b01, b11, b02, b12, b22 = unpack_upper(total)
    w[...] = jnp.zeros((3, N, BLOCK), F32)
    w[0, 0:128, :] = b00
    w[1, 0:128, :] = b01
    w[2, 0:128, :] = b02
    w[1, 128:256, :] = b11
    w[2, 128:256, :] = b12
    extra = (iota((48, 128), 0) == iota((48, 128), 1)) & (iota((48, 128), 0) >= 44)
    w[2, 256:304, :] = jnp.where(extra, 1.0, b22)

    for b, start, stop in SPANS:
        factor_block(w, b, (stop - start) // 8)
        if b < 2:
            later_rows(w, b)
        for t in range(3):
            shape = (stop - start, BLOCK)
            keep = iota(shape, 1) + BLOCK * t <= iota(shape, 0) + start
            linv[start:stop, BLOCK * t:BLOCK * (t + 1)] = jnp.where(keep, w[t, start:stop, :], 0.0)

        @pl.when(has_up)
        def _():
            l_copy(b, start, stop).start()

        if b == 0:
            gather_both()

    outs = []
    high, low = split(linv[...])
    for c, cols in enumerate(columns):
        block = yv[:, cols]
        qv[:, cols] = (nn(high[0:C, 0:C], block) + nn(low[0:C, 0:C], block)).astype(BF16)
        piece = pl.ds(c * CHUNK, CHUNK)
        outs.append(pltpu.make_async_copy(qv.at[:, piece], q_out.at[:, piece], outsem.at[c]))
        outs[-1].start()

    @pl.when(has_down)
    def _():
        for span in SPANS[:2]:
            l_copy(*span).wait_recv()

    def linvp_part(start, stop, index):
        rows = pl.ds(start, stop - start)
        outs.append(pltpu.make_async_copy(linvp.at[rows], linvp_out.at[rows], outsem.at[index]))
        outs[-1].start()

    linvp_part(0, SPANS[1][2], NCH + 2)
    take(total2.at[others], b2)
    outs.append(pltpu.make_async_copy(total2, sums_out, outsem.at[NCH]))
    outs[-1].start()
    cross = total2[:, size_h:, :].reshape(CROSS, BLOCK)
    full[:, 0:128] = cross[0:N]
    full[:, 128:256] = cross[N:2 * N]
    last = cross[2 * N:2 * N + 152]
    left = iota((152, BLOCK), 1) < 64
    full[0:152, 256:384] = jnp.where(left, last, 0.0)
    full[152:304, 256:384] = jnp.where(left, pltpu.roll(last, 64, 1), 0.0)
    right[:, 0:N] = nt(full[...], linv[...], HI)
    right[:, N:] = jnp.zeros((N, LANES - N), F32)
    outs.append(pltpu.make_async_copy(right, right_out, outsem.at[NCH + 1]))
    outs[-1].start()

    @pl.when(has_down)
    def _():
        l_copy(*SPANS[2]).wait_recv()

    linvp_part(*SPANS[2][1:], NCH + 3)
    for copy in outs:
        copy.wait()

    for c in range(NCH):
        @pl.when(has_last)
        def _():
            x_copy(c).wait_send()

        @pl.when(has_next)
        def _():
            c_copy(c).wait_send()

        @pl.when(z_sends)
        def _():
            z_copy(c).wait_send()

    @pl.when(has_up)
    def _():
        for span in SPANS:
            l_copy(*span).wait_send()

    take(recv.at[others], a1)
    take(recv.at[others], a3)
    take(recv_h.at[others], h1)
    take(total2.at[others], b1)

    @pl.when(z_arrives)
    def _():
        take_cross(c1)


def finish_kernel(q_in, sums_in, right_in, linvp_in, q_out, h_out, c_out, sums, right, linvp, full, h, corr, q, sem, q_sem):
    pairs = ((sums_in, sums), (right_in, right), (linvp_in, linvp))
    copies = [pltpu.make_async_copy(*pair, sem.at[i]) for i, pair in enumerate(pairs)]

    def q_copy(source, target, c, way):
        piece = pl.ds(c * CHUNK, CHUNK)
        return pltpu.make_async_copy(source.at[:, piece], target.at[:, piece], q_sem.at[way, c])

    copies[0].start()
    for c in range(NCH):
        q_copy(q_in, q, c, 0).start()
    for copy in copies[1:]:
        copy.start()
    for c in range(NCH):
        q_copy(q_in, q, c, 0).wait()
        q_copy(q, q_out, c, 1).start()
    copies[0].wait()
    size = SYM // sums.shape[0]
    b00, b01, b11, b02, b12, b22 = unpack_upper(sums[:, 0:size, :].reshape(SYM, BLOCK))
    full[0:128, 0:128] = b00
    full[0:128, 128:256] = b01
    full[0:128, 256:384] = b02
    full[128:256, 0:128] = b01.T
    full[128:256, 128:256] = b11
    full[128:256, 256:384] = b12
    full[256:304, 0:128] = b02.T[0:48]
    full[256:304, 128:256] = b12.T[0:48]
    full[256:304, 256:384] = b22
    h[:, 0, :] = full[0:C, 0:C]
    h_copy = pltpu.make_async_copy(h, h_out, sem.at[3])
    h_copy.start()
    copies[1].wait()
    copies[2].wait()
    corr[:, 0, :] = nn(linvp[:, 0:N], right[:, 0:N], HI)[0:C, 0:C]
    c_copy = pltpu.make_async_copy(corr, c_out, sem.at[4])
    c_copy.start()
    for c in range(NCH):
        q_copy(q, q_out, c, 1).wait()
    h_copy.wait()
    c_copy.wait()


def finish(q, sums, right, linvp):
    anywhere = pl.BlockSpec(memory_space=pl.ANY)
    square = jax.ShapeDtypeStruct((C, 1, C), F32)
    return pl.pallas_call(
        finish_kernel, out_shape=(jax.ShapeDtypeStruct((C, ROWS), BF16), square, square),
        in_specs=[anywhere] * 4, out_specs=(anywhere,) * 3,
        scratch_shapes=[pltpu.VMEM(sums.shape, F32)] + [pltpu.VMEM((N, LANES), F32)] * 3
        + [pltpu.VMEM((C, 1, C), F32)] * 2
        + [pltpu.VMEM((C, ROWS), BF16), pltpu.SemaphoreType.DMA((5,)), pltpu.SemaphoreType.DMA((2, NCH))],
        compiler_params=pltpu.CompilerParams(vmem_limit_bytes=57 << 20), name="finish",
    )(q, sums, right, linvp)


def shards(x_block, h_diag, h_right, pattern):
    count, sectors = lax.axis_size("rows"), lax.axis_size("sector")
    dma = pltpu.SemaphoreType.DMA
    vmem = pl.BlockSpec(memory_space=pltpu.VMEM)
    rows_b, square, size = (C, ROWS), (ROWS, ROWS), SYM + CROSS
    q, sums, right, linvp = pl.pallas_call(
        lambda *refs: kernel(count, sectors, *refs),
        out_shape=(jax.ShapeDtypeStruct((C, ROWS), BF16), jax.ShapeDtypeStruct((count, size // count, BLOCK), F32),
                   jax.ShapeDtypeStruct((N, LANES), F32), jax.ShapeDtypeStruct((N, LANES), F32)),
        in_specs=[pl.BlockSpec(memory_space=pltpu.SMEM)] + [pl.BlockSpec(memory_space=pl.ANY)] * 3,
        out_specs=(pl.BlockSpec(memory_space=pl.ANY),) * 4,
        scratch_shapes=[
            pltpu.VMEM(rows_b, BF16), pltpu.VMEM(rows_b, BF16), pltpu.VMEM(square, BF16), pltpu.VMEM(square, BF16),
            pltpu.VMEM(rows_b, F32), pltpu.VMEM(rows_b, BF16), pltpu.VMEM(rows_b, BF16), pltpu.VMEM(rows_b, BF16),
            pltpu.VMEM(rows_b, BF16), pltpu.VMEM((N, LANES), F32),
            pltpu.VMEM((SYM, BLOCK), F32), pltpu.VMEM((count, SYM // count, BLOCK), F32), pltpu.VMEM((SYM, BLOCK), F32),
            pltpu.VMEM((SYM, BLOCK), F32), pltpu.VMEM((count, SYM // count, BLOCK), F32),
            pltpu.VMEM((CROSS, BLOCK), F32), pltpu.VMEM((count, CROSS // count, BLOCK), F32),
            pltpu.VMEM((count, size // count, BLOCK), F32),
            pltpu.VMEM((3, N, BLOCK), F32), pltpu.VMEM((N, LANES), F32), pltpu.VMEM((N, LANES), F32),
            pltpu.VMEM(rows_b, BF16), pltpu.VMEM((N, LANES), F32),
            dma((1 + 2 * NCH,)), dma((NCH,)), dma((NCH,)), dma((NCH,)), dma((NCH,)), dma((NCH,)), dma((NCH,)),
            dma((3,)), dma((3,)), dma((NCH + 4,)),
        ] + [dma] * 10,
        compiler_params=pltpu.CompilerParams(collective_id=0, has_side_effects=True, vmem_limit_bytes=57 << 20),
        name="step",
    )(jnp.swapaxes(pattern[0], 0, 1), x_block[0].T, h_diag[0], h_right[0])
    q, h, corr = finish(q, sums, right, linvp)
    return q.T[None], jnp.swapaxes(h, 0, 1), jnp.swapaxes(corr, 0, 1)


def solution(mesh):
    in_specs = (
        P("sector", "rows", None),
        P("sector", "rows", None),
        P("sector", "rows", None),
        P("sector", None, "rows", None),
    )
    out_specs = (P("sector", "rows", None), P("sector", None, None), P("sector", None, None))
    return jax.shard_map(shards, mesh=mesh, in_specs=in_specs, out_specs=out_specs, check_vma=False)
```
